128 devices in a mesh: row: 4 (over z_lo, core), basis: 8 (over z_hi, y), rep: 4 (over x).
Axes of the slice: x: 4, y: 4, z: 4 (z_hi: 2, z_lo: 2; z = z_hi * 2 + z_lo), core: 2. Of those that a mesh axis runs over, the one named last changes fastest.
Arguments:
- blocks: float32 [3072, 7, 128, 128], P(('row', 'basis', 'rep')), as said below
- pattern: int32 [3072, 7], P(('row', 'basis', 'rep')), may hold values from 0 to 3071, as said below
- counts: int32 [3072], P(('row', 'basis', 'rep')), may hold values from 1 to 7, as said below
- stored: float32 [512, 393216], P(None, ('row', 'basis', 'rep')), as said below
- start_block: float32 [64, 393216], P(None, ('row', 'basis', 'rep')), may hold values from -6 to 6, as said below
Outputs:
- diagonal_blocks: float32 [2, 64, 64], replicated
- coupling_blocks: float32 [2, 64, 64], replicated
- last_block: float32 [64, 393216], P(None, ('row', 'basis', 'rep'))
The draws below stay inside these ranges and needn't reach their ends.
Inputs may be any that keep to these rules, and one draw needn't show every extreme that they name: `pattern`: the first counts[i] entries of row block i are distinct column blocks j with (j - i) mod 3072 at most 24 or at least 3048; the used entries are symmetric (i uses j exactly when j uses i); the other entries are column blocks within the same reach. `counts`: the number of used slots of each row block; some row block uses all 7. The used blocks form a symmetric matrix: the block of row block i at column block j is the transpose of that of j at i. `stored`: real entries of order one over the square root of 393216. `start_block`: real entries of order one.
All inputs are finite; a program needn't handle non-finite values.
Results may differ from the reference program's by a relative error of at most 0.00016.
Values sent between devices are 32-bit elements; how exact they have to be, the bound alone decides.
No kernel may reach another device: no remote copies, remote signals or barrier semaphores. Data moves between devices by JAX's collectives and lax.ppermute only.
A program may use at most 128 MiB of HBM per device.

```python
import math
import jax
import jax.numpy as jnp
from jax import lax

BS = 128
BW = 64
KS = 512
NZ = 7
ITERS = 2
NBD = 24
NB = 3072
NROWS = 393216


def layout(key):
    half_count = (NZ - 1) // 2
    perm_key = jax.random.fold_in(key, 11)
    keep_key = jax.random.fold_in(key, 12)
    offsets = jax.random.permutation(perm_key, NBD)[:half_count].astype(jnp.int32) + 1
    keep_table = jax.random.randint(keep_key, (NB, half_count), 0, 4) != 0
    row_ids = jnp.arange(NB, dtype=jnp.int32)[:, None]
    upper_col = (row_ids + offsets[None, :]) % NB
    lower_col = (row_ids - offsets[None, :]) % NB
    keep_upper = keep_table | (row_ids == 0) | (upper_col == 0)
    keep_lower = keep_table[lower_col, jnp.arange(half_count)[None, :]] | (row_ids == 0) | (lower_col == 0)
    candidates = jnp.concatenate([row_ids, jnp.stack([upper_col, lower_col], axis=2).reshape(NB, 2 * half_count)], axis=1)
    keep_flags = jnp.stack([keep_upper, keep_lower], axis=2).reshape(NB, 2 * half_count).astype(jnp.int32)
    keep_all = jnp.concatenate([jnp.ones((NB, 1), jnp.int32), keep_flags], axis=1)
    slot_order = jnp.argsort(1 - keep_all, axis=1, stable=True).astype(jnp.int32)
    pattern = jnp.take_along_axis(candidates, slot_order, axis=1).astype(jnp.int32)
    counts = jnp.sum(keep_all, axis=1).astype(jnp.int32)
    return (pattern, counts, slot_order, lower_col)


def draw_pattern(key, part):
    return layout(key)[0]


def draw_counts(key, part):
    return layout(key)[1]


def draw_blocks(key, part):
    pattern, counts, slot_order, lower_col = layout(key)
    half_count = (NZ - 1) // 2
    pair_key = jax.random.fold_in(key, 13)
    diag_key = jax.random.fold_in(key, 14)
    scale_key = jax.random.fold_in(key, 15)
    pair_table = jax.random.normal(pair_key, (NB, half_count, BS, BS), jnp.float32)
    diag_table = jax.random.normal(diag_key, (NB, BS, BS), jnp.float32)
    state_scale = jnp.exp(jax.random.uniform(scale_key, (NB, BS), jnp.float32, 0.0, math.log(10.0)))
    diag_blocks = (diag_table + jnp.swapaxes(diag_table, 1, 2)) * math.sqrt(0.5)
    lower_blocks = jnp.swapaxes(pair_table[lower_col, jnp.arange(half_count)[None, :]], 2, 3)
    paired = jnp.stack([pair_table, lower_blocks], axis=2).reshape(NB, 2 * half_count, BS, BS)
    candidate_blocks = jnp.concatenate([diag_blocks[:, None], paired], axis=1)
    chosen = jnp.take_along_axis(candidate_blocks, slot_order[:, :, None, None], axis=1)
    column_scale = state_scale[pattern]
    factor = 1.0 / (5.0 * math.sqrt(NZ * BS))
    return chosen * state_scale[:, None, :, None] * column_scale[:, :, None, :] * factor


def shared_rows(key):
    common_key = jax.random.fold_in(key, 31)
    return jnp.clip(jax.random.normal(common_key, (BW, NROWS), jnp.float32), -4.0, 4.0)


def draw_stored(key, part):
    common = shared_rows(key)
    key = jax.random.fold_in(key, 21)
    rest_key = jax.random.fold_in(key, 1)
    scale_key = jax.random.fold_in(key, 2)
    others = jnp.clip(jax.random.normal(rest_key, (KS - BW, NROWS), jnp.float32), -4.0, 4.0)
    row_scale = jax.random.uniform(scale_key, (KS,), jnp.float32, 0.75, 1.25)
    table = jnp.concatenate([common, others], axis=0)
    return table * row_scale[:, None] * (1.0 / math.sqrt(NROWS))


def draw_start_block(key, part):
    common = shared_rows(key)
    key = jax.random.fold_in(key, 22)
    noise = jnp.clip(jax.random.normal(key, (BW, NROWS), jnp.float32), -4.0, 4.0)
    return jnp.clip(noise + common, -6.0, 6.0)


def setup_inputs(seed: int = 0) -> dict:
    arg_keys = jax.random.split(jax.random.key(seed), 6)
    return {
        "blocks": draw_blocks(jax.random.fold_in(arg_keys[5], 71), 0),
        "pattern": draw_pattern(jax.random.fold_in(arg_keys[5], 71), 0),
        "counts": draw_counts(jax.random.fold_in(arg_keys[5], 71), 0),
        "stored": draw_stored(jax.random.fold_in(arg_keys[5], 71), 0),
        "start_block": draw_start_block(jax.random.fold_in(arg_keys[5], 71), 0),
    }


precise = lax.Precision.HIGHEST

def times_transposed(left, right):
    return lax.dot_general(left.astype(jnp.float32), right.astype(jnp.float32), (((1,), (1,)), ((), ())), precision=precise, preferred_element_type=jnp.float32)

def combine_rows(coeffs, rows):
    return lax.dot_general(coeffs.astype(jnp.float32), rows.astype(jnp.float32), (((0,), (0,)), ((), ())), precision=precise, preferred_element_type=jnp.float32)

def remove_parts(target, stored, current, previous, part_stored, part_current, part_previous):
    target = target - combine_rows(part_stored, stored)
    target = target - combine_rows(part_current, current)
    return target - combine_rows(part_previous, previous)

def finish(residue, gram):
    factor = jnp.linalg.cholesky(gram)
    return (lax.linalg.triangular_solve(factor, residue, left_side=True, lower=True), factor)

def apply_operator(blocks, pattern, counts, panel_rows):
    columns = panel_rows.shape[0]
    row_blocks = blocks.shape[0]
    slots = blocks.shape[1]
    block_size = blocks.shape[2]
    tile_set = panel_rows.reshape(columns, row_blocks, block_size)[:, pattern]
    in_use = (jnp.arange(slots, dtype=jnp.int32)[None, :] < counts[:, None]).astype(panel_rows.dtype)
    tile_set = tile_set * in_use[None, :, :, None]
    result = jnp.einsum('isab,cisb->cia', blocks, tile_set, precision=precise)
    return result.reshape(columns, row_blocks * block_size)

def orthonormalize(image_block, stored, current, previous):
    stored_one = times_transposed(stored, image_block)
    current_one = times_transposed(current, image_block)
    previous_one = times_transposed(previous, image_block)
    residue = remove_parts(image_block, stored, current, previous, stored_one, current_one, previous_one)
    stored_two = times_transposed(stored, residue)
    current_two = times_transposed(current, residue)
    previous_two = times_transposed(previous, residue)
    final = remove_parts(residue, stored, current, previous, stored_two, current_two, previous_two)
    gram = times_transposed(final, final)
    following, factor = finish(final, gram)
    return (following, factor, current_one + current_two)

def reference(blocks, pattern, counts, stored, start_block):
    zero_block = jnp.zeros_like(start_block)
    current, factor, coeffs = orthonormalize(start_block, stored, zero_block, zero_block)
    previous = zero_block
    diagonal_parts = []
    coupling_parts = []
    for iteration in range(ITERS):
        image_block = apply_operator(blocks, pattern, counts, current)
        following, factor, coeffs = orthonormalize(image_block, stored, current, previous)
        diagonal_parts.append(coeffs)
        coupling_parts.append(factor.T)
        previous = current
        current = following
    return (jnp.stack(diagonal_parts), jnp.stack(coupling_parts), current * math.sqrt(NROWS))
```

```python
import functools
import math

import jax
import jax.numpy as jnp
from jax import lax
from jax.experimental import pallas as pl
from jax.experimental.pallas import tpu as pltpu
from jax.sharding import PartitionSpec as P

AXES = ("row", "basis", "rep")
HIGH = lax.Precision.HIGH
FULL = lax.Precision.HIGHEST
F32 = jnp.float32
BF16 = jnp.bfloat16
RB = 2


def dot_nt(a, b, precision=FULL):
    return lax.dot_general(a, b, (((1,), (1,)), ((), ())), precision=precision, preferred_element_type=F32)


def dot_tn(a, b, precision=FULL):
    return lax.dot_general(a, b, (((0,), (0,)), ((), ())), precision=precision, preferred_element_type=F32)


def dot_nn(a, b, precision=FULL):
    return lax.dot_general(a, b, (((1,), (0,)), ((), ())), precision=precision, preferred_element_type=F32)


def total(x):
    n = lax.axis_size(AXES)
    parts = lax.all_to_all(x.reshape(n, x.size // n), AXES, 0, 0, tiled=True)
    mine = jnp.sum(parts, axis=0)
    out = lax.all_to_all(jnp.broadcast_to(mine[None], parts.shape), AXES, 0, 0, tiled=True)
    return out.reshape(x.shape)


def split(x):
    hi = x.astype(BF16)
    lo = (x - hi.astype(F32)).astype(BF16)
    return hi, lo


def bdot_nt(a, b):
    return lax.dot_general(a, b, (((1,), (1,)), ((), ())), preferred_element_type=F32)


def apply_kernel(cols, blocks, stored, left, mid, right, prev, u_out, m_out, pieces, acc, accw, accp, *, nbd, with_prev):
    step = pl.program_id(0)
    slots = blocks.shape[1]
    bs = blocks.shape[2]
    bw = mid.shape[0]

    @pl.when(step == 0)
    def _():
        pieces[3 * nbd] = jnp.zeros((2 * bw, bs), BF16)
        for k, src in enumerate((left, mid, right)):
            for b in range(nbd):
                hi, lo = split(src[:, b * bs : (b + 1) * bs])
                pieces[k * nbd + b] = jnp.concatenate([hi, lo], axis=0)
        acc[...] = jnp.zeros_like(acc)
        accw[...] = jnp.zeros_like(accw)
        accp[...] = jnp.zeros_like(accp)

    his = []
    for r in range(RB):
        i = step * RB + r
        tot = jnp.zeros((2 * bw, bs), F32)
        for s in range(slots):
            j = cols[i * slots + s]
            v = pieces[j]
            ahi, alo = split(blocks[r, s])
            tot = tot + bdot_nt(v, ahi) + bdot_nt(v, alo)
        u = tot[:bw] + tot[bw:]
        u_out[:, r * bs : (r + 1) * bs] = u
        hi, lo = split(u)
        his.append(jnp.concatenate([hi, lo], axis=0))
    u2 = jnp.concatenate(his, axis=1)
    shi, slo = split(stored[...])
    acc[...] += bdot_nt(shi, u2) + bdot_nt(slo, u2)
    start = pl.multiple_of(step * (RB * bs), RB * bs)
    rows = list(split(mid[:, pl.ds(start, RB * bs)]))
    both = jnp.concatenate([u2] + rows, axis=0)
    accw[...] += bdot_nt(rows[0], both) + bdot_nt(rows[1], both)
    if with_prev:
        rows = list(split(prev[:, pl.ds(start, RB * bs)]))
        accp[...] += bdot_nt(rows[0], u2) + bdot_nt(rows[1], u2)

    @pl.when(step == pl.num_programs(0) - 1)
    def _():
        ks = acc.shape[0]
        a = acc[:, :bw] + acc[:, bw:]
        m_out[: ks // 2, :bw] = a[: ks // 2]
        m_out[: ks // 2, bw:] = a[ks // 2 :]
        for k in range(2):
            w = accw[:, 2 * bw * k : 2 * bw * (k + 1)]
            m_out[ks // 2 : ks // 2 + bw, bw * k : bw * (k + 1)] = w[:, :bw] + w[:, bw:]
        if with_prev:
            p = accp[:, :bw] + accp[:, bw:]
            m_out[ks // 2 + bw :, :bw] = p[: bw // 2]
            m_out[ks // 2 + bw :, bw:] = p[bw // 2 :]


def apply_op(cols, blocks, stored, left, mid, right, prev, with_prev):
    nbd, slots, bs, _ = blocks.shape
    bw, n = mid.shape
    ks = stored.shape[0]
    rows = ks // 2 + bw + (bw // 2 if with_prev else 0)
    whole = pl.BlockSpec((bw, n), lambda i, c: (0, 0))
    return pl.pallas_call(
        functools.partial(apply_kernel, nbd=nbd, with_prev=with_prev),
        grid_spec=pltpu.PrefetchScalarGridSpec(
            num_scalar_prefetch=1,
            grid=(nbd // RB,),
            in_specs=[
                pl.BlockSpec((RB, slots, bs, bs), lambda i, c: (i, 0, 0, 0)),
                pl.BlockSpec((ks, RB * bs), lambda i, c: (0, i)),
                whole,
                whole,
                whole,
                whole,
            ],
            out_specs=[
                pl.BlockSpec((bw, RB * bs), lambda i, c: (0, i)),
                pl.BlockSpec((rows, 2 * bw), lambda i, c: (0, 0)),
            ],
            scratch_shapes=[
                pltpu.VMEM((3 * nbd + 1, 2 * bw, bs), BF16),
                pltpu.VMEM((ks, 2 * bw), F32),
                pltpu.VMEM((bw, 4 * bw), F32),
                pltpu.VMEM((bw, 2 * bw), F32),
            ],
        ),
        out_shape=[
            jax.ShapeDtypeStruct((bw, n), F32),
            jax.ShapeDtypeStruct((rows, 2 * bw), F32),
        ],
        compiler_params=pltpu.CompilerParams(vmem_limit_bytes=48 * 1024 * 1024),
        name="apply_op",
    )(cols, blocks, stored, left, mid, right, prev)


def factor_of(gram):
    low = jnp.linalg.cholesky(gram)
    inv = lax.linalg.triangular_solve(low, jnp.eye(gram.shape[0], dtype=F32), left_side=True, lower=True)
    return low, inv


def on_device(blocks, pattern, counts, stored, start_block):
    nbd, slots, bs, _ = blocks.shape
    bw, n = start_block.shape
    ks = stored.shape[0]
    half = ks // 2
    devices = lax.axis_size(AXES)
    position = lax.axis_index(AXES)
    nb = nbd * devices
    local = (pattern - (position - 1) * nbd) % nb
    used = jnp.arange(slots, dtype=jnp.int32)[None, :] < counts[:, None]
    cols = jnp.where(used, local, 3 * nbd).reshape(-1)
    up = [(i, (i + 1) % devices) for i in range(devices)]
    down = [(j, i) for i, j in up]

    def halo(w):
        return lax.ppermute(w, AXES, up), lax.ppermute(w, AXES, down)

    top = dot_nt(stored[:half], stored, HIGH)
    corner = dot_nt(stored[half:], stored[half:], HIGH)
    first = dot_nt(stored, start_block, HIGH)
    packed = total(jnp.concatenate([top, corner, first[:half], first[half:]], axis=1))
    s11, s12, s22 = packed[:, :half], packed[:, half:ks], packed[:, ks : ks + half]
    c1 = jnp.concatenate([packed[:, ks + half : ks + half + bw], packed[:, ks + half + bw :]], axis=0)

    def times_s(c):
        a, b = c[:half], c[half:]
        return jnp.concatenate([dot_nn(s11, a) + dot_nn(s12, b), dot_tn(s12, a) + dot_nn(s22, b)], axis=0)

    def unpack(m):
        ms = jnp.concatenate([m[:half, :bw], m[:half, bw:]], axis=0)
        return ms, m[half : half + bw, :bw], m[half : half + bw, bw:]

    d = 2.0 * c1 - times_s(c1)
    w1 = start_block - dot_tn(d, stored, HIGH)
    c3 = c1 - times_s(d)

    left, right = halo(w1)
    u1, m1 = apply_op(cols, blocks, stored, left, w1, right, w1, False)
    ms, h, g = unpack(total(m1))
    l1, e1 = factor_of(g)
    k1 = dot_nt(c3, e1)
    c1s = dot_nt(ms, e1)
    c1v = dot_nt(dot_nn(e1, h), e1)
    c2s = c1s - times_s(c1s) - dot_nn(k1, c1v)
    c2v = -dot_tn(k1, c1s)
    ds = c1s + c2s
    dv = c1v + c2v
    diag1 = dv
    w2 = dot_nn(e1, u1, HIGH) - dot_tn(ds, stored, HIGH) - dot_nn(dot_tn(dv, e1), w1, HIGH)
    c3s = c2s - times_s(c2s) - dot_nn(k1, c2v)
    c3v = -dot_tn(k1, c2s)

    left, right = halo(w2)
    u2, m2 = apply_op(cols, blocks, stored, left, w2, right, w1, True)
    m2 = total(m2)
    ms, h, g = unpack(m2)
    h12 = jnp.concatenate([m2[half + bw :, :bw], m2[half + bw :, bw:]], axis=0)
    l2, e2 = factor_of(g)
    k2 = dot_nt(c3s, e2)
    n12 = dot_nt(c3v, e2)
    c1s = dot_nt(ms, e2)
    c1a = dot_nt(dot_nn(e2, h), e2)
    c1b = dot_nt(dot_nn(e1, h12), e2)
    ds = 2.0 * c1s - times_s(c1s) - dot_nn(k2, c1a) - dot_nn(k1, c1b)
    da = c1a - dot_tn(k2, c1s) - dot_tn(n12, c1b)
    db = c1b - dot_tn(k1, c1s) - dot_nn(n12, c1a)
    w3 = (
        dot_nn(e2, u2, HIGH)
        - dot_tn(ds, stored, HIGH)
        - dot_nn(dot_tn(da, e2), w2, HIGH)
        - dot_nn(dot_tn(db, e1), w1, HIGH)
    )
    g3 = total(dot_nt(w3, w3, HIGH).reshape(bw // 2, 2 * bw)).reshape(bw, bw)
    l3, e3 = factor_of(g3)
    last = dot_nn(e3 * math.sqrt(nb * bs), w3, HIGH)
    return jnp.stack([diag1, da]), jnp.stack([l2.T, l3.T]), last


def solution(mesh):
    in_specs = (
        P(AXES, None, None, None),
        P(AXES, None),
        P(AXES),
        P(None, AXES),
        P(None, AXES),
    )
    out_specs = (P(), P(), P(None, AXES))
    return jax.shard_map(on_device, mesh=mesh, in_specs=in_specs, out_specs=out_specs, check_vma=False)
```

```python
import functools
import math

import jax
import jax.numpy as jnp
from jax import lax
from jax.experimental import pallas as pl
from jax.experimental.pallas import tpu as pltpu
from jax.sharding import PartitionSpec as P

AXES = ("row", "basis", "rep")
HIGH = lax.Precision.HIGH
FULL = lax.Precision.HIGHEST
F32 = jnp.float32
BF16 = jnp.bfloat16
RB = 2
TILE = 768
VMEM_LIMIT = 48 * 1024 * 1024


def dot_nt(a, b, precision=FULL):
    return lax.dot_general(a, b, (((1,), (1,)), ((), ())), precision=precision, preferred_element_type=F32)


def dot_tn(a, b, precision=FULL):
    return lax.dot_general(a, b, (((0,), (0,)), ((), ())), precision=precision, preferred_element_type=F32)


def dot_nn(a, b, precision=FULL):
    return lax.dot_general(a, b, (((1,), (0,)), ((), ())), precision=precision, preferred_element_type=F32)


def bdot(a, b):
    return jnp.dot(a, b, preferred_element_type=F32)


def total(x):
    n = lax.axis_size(AXES)
    parts = lax.all_to_all(x.reshape(n, x.size // n), AXES, 0, 0, tiled=True)
    mine = jnp.sum(parts, axis=0)
    out = lax.all_to_all(jnp.broadcast_to(mine[None], parts.shape), AXES, 0, 0, tiled=True)
    return out.reshape(x.shape)


def split(x):
    hi = x.astype(BF16)
    lo = (x - hi.astype(F32)).astype(BF16)
    return hi, lo


def turned(x):
    hi = x.astype(BF16).astype(F32)
    return jnp.concatenate([hi, x - hi], axis=0).T.astype(BF16)


def apply_kernel(cols, blocks, stored, left, mid, right, prev, u_out, m_out, pieces, acc, accw, *, nbd):
    step = pl.program_id(0)
    slots = blocks.shape[1]
    bs = blocks.shape[2]
    bw = mid.shape[0]

    @pl.when(step == 0)
    def _():
        pieces[3 * nbd] = jnp.zeros((2 * bs, 2 * bw), BF16)
        for k, src in enumerate((left, mid, right)):
            for b in range(nbd):
                t = turned(src[:, b * bs : (b + 1) * bs])
                pieces[k * nbd + b, :bs] = t
                pieces[k * nbd + b, bs:] = t
        acc[...] = jnp.zeros_like(acc)
        accw[...] = jnp.zeros_like(accw)

    us, uts = [], []
    for r in range(RB):
        i = step * RB + r
        tot = None
        for s in range(slots):
            both = jnp.concatenate(split(blocks[r, s]), axis=1)
            part = bdot(both, pieces[cols[i * slots + s]])
            tot = part if tot is None else tot + part
        t = tot.T
        u = t[:bw] + t[bw:]
        u_out[:, r * bs : (r + 1) * bs] = u
        us.append(u)
        uts.append(turned(u))
    u = jnp.concatenate(us, axis=1)
    ut = jnp.concatenate(uts, axis=0)
    shi, slo = split(stored[...])
    acc[...] += bdot(shi, ut) + bdot(slo, ut)
    wt = jnp.concatenate([pieces[nbd + step * RB + r, :bs] for r in range(RB)], axis=0)
    both = jnp.concatenate([ut, wt], axis=1)
    start = pl.multiple_of(step * (RB * bs), RB * bs)
    here = pl.ds(start, RB * bs)
    rhi, rlo = split(jnp.concatenate([mid[:, here], prev[:, here], u], axis=0))
    accw[...] += bdot(rhi, both) + bdot(rlo, both)

    @pl.when(step == pl.num_programs(0) - 1)
    def _():
        ks = acc.shape[0]
        t = acc[...].T
        a = t[:bw] + t[bw:]
        m_out[:bw, : ks // 2] = a[:, : ks // 2]
        m_out[bw:, : ks // 2] = a[:, ks // 2 :]
        w = accw[...]
        wu = w[:, :bw] + w[:, bw : 2 * bw]
        ww = w[:bw, 2 * bw : 3 * bw] + w[:bw, 3 * bw :]
        m_out[:bw, ks // 2 :] = jnp.concatenate([wu[:bw], ww], axis=1)
        m_out[bw:, ks // 2 :] = jnp.concatenate([wu[bw : 2 * bw], wu[2 * bw :]], axis=1)


def apply_op(cols, blocks, stored, left, mid, right, prev):
    nbd, slots, bs, _ = blocks.shape
    bw, n = mid.shape
    ks = stored.shape[0]
    whole = pl.BlockSpec((bw, n), lambda i, c: (0, 0))
    return pl.pallas_call(
        functools.partial(apply_kernel, nbd=nbd),
        grid_spec=pltpu.PrefetchScalarGridSpec(
            num_scalar_prefetch=1,
            grid=(nbd // RB,),
            in_specs=[
                pl.BlockSpec((RB, slots, bs, bs), lambda i, c: (i, 0, 0, 0)),
                pl.BlockSpec((ks, RB * bs), lambda i, c: (0, i)),
                whole,
                whole,
                whole,
                whole,
            ],
            out_specs=[
                pl.BlockSpec((bw, RB * bs), lambda i, c: (0, i)),
                pl.BlockSpec((2 * bw, ks // 2 + 2 * bw), lambda i, c: (0, 0)),
            ],
            scratch_shapes=[
                pltpu.VMEM((3 * nbd + 1, 2 * bs, 2 * bw), BF16),
                pltpu.VMEM((ks, 2 * bw), F32),
                pltpu.VMEM((3 * bw, 4 * bw), F32),
            ],
        ),
        out_shape=[
            jax.ShapeDtypeStruct((bw, n), F32),
            jax.ShapeDtypeStruct((2 * bw, ks // 2 + 2 * bw), F32),
        ],
        compiler_params=pltpu.CompilerParams(vmem_limit_bytes=VMEM_LIMIT),
        name="apply_op",
    )(cols, blocks, stored, left, mid, right, prev)


def project_kernel(cs, cw, stored, *refs):
    arrays, out = refs[:-1], refs[-1]
    bw = cs.shape[0]
    chi, clo = split(jnp.concatenate([cs[...], cw[...]], axis=1))
    dhi, dlo = split(jnp.concatenate([stored[...]] + [a[...] for a in arrays], axis=0))
    t = bdot(jnp.concatenate([chi, clo], axis=0), dhi)
    out[...] = t[:bw] + t[bw:] + bdot(chi, dlo)


def project(cs, cw, stored, *arrays):
    ks, n = stored.shape
    bw = cs.shape[0]
    return pl.pallas_call(
        project_kernel,
        grid=(n // TILE,),
        in_specs=[
            pl.BlockSpec(cs.shape, lambda i: (0, 0)),
            pl.BlockSpec(cw.shape, lambda i: (0, 0)),
            pl.BlockSpec((ks, TILE), lambda i: (0, i)),
        ]
        + [pl.BlockSpec((bw, TILE), lambda i: (0, i))] * len(arrays),
        out_specs=pl.BlockSpec((bw, TILE), lambda i: (0, i)),
        out_shape=jax.ShapeDtypeStruct((bw, n), F32),
        compiler_params=pltpu.CompilerParams(vmem_limit_bytes=VMEM_LIMIT),
        name="project",
    )(cs, cw, stored, *arrays)


PANEL = 4


def factor_of(gram):
    n = gram.shape[0]
    row = lax.broadcasted_iota(jnp.int32, (n, 2 * n), 0)
    lane = lax.broadcasted_iota(jnp.int32, (n, 2 * n), 1)
    eye = (lane == row + n).astype(F32)
    m = jnp.where(lane < n, jnp.concatenate([gram, gram], axis=1), eye)
    scale = jnp.zeros((n, 2 * n), F32)
    for p in range(0, n, PANEL):
        cols = [jnp.broadcast_to(m[:, p + j : p + j + 1], (n, 2 * n)) for j in range(PANEL)]
        for j in range(PANEL):
            k = p + j
            pivot = cols[j][k : k + 1]
            root = lax.rsqrt(pivot)
            root = root * (1.5 - 0.5 * pivot * root * root)
            f = jnp.where(row > k, cols[j] * (root * root), 0.0)
            scale = jnp.where(row == k, root, scale)
            m = m - f * m[k : k + 1]
            for q in range(j + 1, PANEL):
                cols[q] = cols[q] - f * cols[q][k : k + 1]
    m = m * scale
    upper = jnp.where(lane >= row, m, 0.0)[:, :n]
    return upper, m[:, n:]


def unpacked(t, bw):
    half = t.shape[1] - 2 * bw
    mst = jnp.concatenate([t[:bw, :half], t[bw:, :half]], axis=1)
    a = t[:bw, half:]
    b = t[bw:, half:]
    return mst, a[:, :bw], a[:, bw:], b[:, :bw], b[:, bw:]


def second_kernel(t, s, c3t, cs, cw, diag, upper, e_out, k_out, c2t_out, c2vt_out):
    bw = c3t.shape[0]
    mst, h, g, _, _ = unpacked(t[...], bw)
    _, e1 = factor_of(g)
    k1t = dot_nn(e1, c3t[...])
    c1t = dot_nn(e1, mst)
    c1vt = dot_nt(e1, dot_nn(e1, h))
    c2t = c1t - dot_nn(c1t, s[...]) - dot_nn(c1vt, k1t)
    c2vt = -dot_nt(c1t, k1t)
    dvt = c1vt + c2vt
    cs[...] = -(c1t + c2t)
    cw[...] = jnp.concatenate([e1, -dot_nn(dvt, e1)], axis=1)
    diag[...] = dvt.T
    upper[...] = jnp.zeros_like(upper)
    e_out[...] = e1
    k_out[...] = k1t
    c2t_out[...] = c2t
    c2vt_out[...] = c2vt


def after_kernel(s, k1t, c2t, c2vt, c3st, c3vt):
    c3st[...] = c2t[...] - dot_nn(c2t[...], s[...]) - dot_nn(c2vt[...], k1t[...])
    c3vt[...] = -dot_nt(c2t[...], k1t[...])


def third_kernel(t, s, c3st, c3vt, k1t_ref, e1_ref, cs, cw, diag, upper2, upper3, *, size):
    bw = c3st.shape[0]
    k1t, e1, sm = k1t_ref[...], e1_ref[...], s[...]
    mst, h, g, h12, uu = unpacked(t[...], bw)
    lt2, e2 = factor_of(g)
    upper2[...] = lt2
    k2t = dot_nn(e2, c3st[...])
    n12t = dot_nn(e2, c3vt[...])
    c1t = dot_nn(e2, mst)
    c1at = dot_nt(e2, dot_nn(e2, h))
    c1bt = dot_nt(e2, dot_nn(e1, h12))
    yy = dot_nt(dot_nn(e2, uu), e2)
    dst = 2.0 * c1t - dot_nn(c1t, sm) - dot_nn(c1at, k2t) - dot_nn(c1bt, k1t)
    dat = c1at - dot_nt(c1t, k2t) - dot_nt(c1bt, n12t)
    dbt = c1bt - dot_nt(c1t, k1t) - dot_nn(c1at, n12t)
    diag[...] = dat.T
    c3s = c1t - dot_nn(dst, sm) - dot_nn(dat, k2t) - dot_nn(dbt, k1t)
    c3a = c1at - dot_nt(dst, k2t) - dat - dot_nt(dbt, n12t)
    c3b = c1bt - dot_nt(dst, k1t) - dot_nn(dat, n12t) - dbt
    g3 = yy - dot_nt(c1t, dst) - dot_nt(dst, c3s)
    g3 = g3 - dot_nt(c1at, dat) - dot_nt(dat, c3a) - dot_nt(c1bt, dbt) - dot_nt(dbt, c3b)
    lt3, e3 = factor_of(0.5 * (g3 + g3.T))
    upper3[...] = lt3
    e3 = e3 * math.sqrt(size)
    cs[...] = -dot_nn(e3, dst)
    cw[...] = jnp.concatenate(
        [dot_nn(e3, e2), -dot_nn(e3, dot_nn(dat, e2)), -dot_nn(e3, dot_nn(dbt, e1))], axis=1
    )


def small(kernel, name, shapes, *args):
    return pl.pallas_call(
        kernel,
        out_shape=[jax.ShapeDtypeStruct(s, F32) for s in shapes],
        compiler_params=pltpu.CompilerParams(vmem_limit_bytes=VMEM_LIMIT),
        name=name,
    )(*args)


def on_device(blocks, pattern, counts, stored, start_block):
    nbd, slots, bs, _ = blocks.shape
    bw, n = start_block.shape
    ks = stored.shape[0]
    half = ks // 2
    devices = lax.axis_size(AXES)
    position = lax.axis_index(AXES)
    nb = nbd * devices
    local = (pattern - (position - 1) * nbd) % nb
    used = jnp.arange(slots, dtype=jnp.int32)[None, :] < counts[:, None]
    cols = jnp.where(used, local, 3 * nbd).reshape(-1)
    up = [(i, (i + 1) % devices) for i in range(devices)]
    down = [(j, i) for i, j in up]

    def halo(w):
        return lax.ppermute(w, AXES, up), lax.ppermute(w, AXES, down)

    top = dot_nt(stored[:half], stored, HIGH)
    corner = dot_nt(stored[half:], stored[half:], HIGH)
    first = dot_nt(stored, start_block, HIGH)
    packed = total(jnp.concatenate([top, corner, first[:half], first[half:]], axis=1))
    s12 = packed[:, half:ks]
    s = jnp.concatenate(
        [packed[:, :ks], jnp.concatenate([s12.T, packed[:, ks : ks + half]], axis=1)], axis=0
    )
    c1 = jnp.concatenate([packed[:, ks + half : ks + half + bw], packed[:, ks + half + bw :]], axis=0)
    c1t = c1.T
    dt = 2.0 * c1t - dot_nn(c1t, s)
    w1 = project(-dt, jnp.eye(bw, dtype=F32), stored, start_block)
    c3t = c1t - dot_nn(dt, s)

    left, right = halo(w1)
    u1, m1 = apply_op(cols, blocks, stored, left, w1, right, w1)
    sq, wide = (bw, bw), (bw, ks)
    cs, cw, diag1, _, e1, k1t, c2t, c2vt = small(
        second_kernel, "second", [wide, (bw, 2 * bw), sq, sq, sq, wide, wide, sq], total(m1), s, c3t
    )
    w2 = project(cs, cw, stored, u1, w1)
    c3st, c3vt = small(after_kernel, "after", [wide, sq], s, k1t, c2t, c2vt)

    left, right = halo(w2)
    u2, m2 = apply_op(cols, blocks, stored, left, w2, right, w1)
    cs, cw, diag2, upper2, upper3 = small(
        functools.partial(third_kernel, size=nb * bs),
        "third",
        [wide, (bw, 3 * bw), sq, sq, sq],
        total(m2), s, c3st, c3vt, k1t, e1,
    )
    last = project(cs, cw, stored, u2, w2, w1)
    return jnp.stack([diag1, diag2]), jnp.stack([upper2, upper3]), last


def solution(mesh):
    in_specs = (
        P(AXES, None, None, None),
        P(AXES, None),
        P(AXES),
        P(None, AXES),
        P(None, AXES),
    )
    out_specs = (P(), P(), P(None, AXES))
    return jax.shard_map(on_device, mesh=mesh, in_specs=in_specs, out_specs=out_specs, check_vma=False)
```

```python
import functools
import math

import jax
import jax.numpy as jnp
from jax import lax
from jax.experimental import pallas as pl
from jax.experimental.pallas import tpu as pltpu
from jax.sharding import PartitionSpec as P

AXES = ("row", "basis", "rep")
HIGH = lax.Precision.HIGH
FULL = lax.Precision.HIGHEST
F32 = jnp.float32
BF16 = jnp.bfloat16
RB = 4
CHUNK = 4
TILE = 512
VMEM_LIMIT = 12 * 1024 * 1024


def dot_nt(a, b, precision=FULL):
    return lax.dot_general(a, b, (((1,), (1,)), ((), ())), precision=precision, preferred_element_type=F32)


def dot_tn(a, b, precision=FULL):
    return lax.dot_general(a, b, (((0,), (0,)), ((), ())), precision=precision, preferred_element_type=F32)


def dot_nn(a, b, precision=FULL):
    return lax.dot_general(a, b, (((1,), (0,)), ((), ())), precision=precision, preferred_element_type=F32)


def bdot(a, b):
    return jnp.dot(a, b, preferred_element_type=F32)


def total(x):
    n = lax.axis_size(AXES)
    parts = lax.all_to_all(x.reshape(n, x.size // n), AXES, 0, 0, tiled=True)
    mine = jnp.sum(parts, axis=0)
    out = lax.all_to_all(jnp.broadcast_to(mine[None], parts.shape), AXES, 0, 0, tiled=True)
    return out.reshape(x.shape)


def split(x):
    hi = x.astype(BF16)
    lo = (x - hi.astype(F32)).astype(BF16)
    return hi, lo


def turned(x):
    hi = x.astype(BF16).astype(F32)
    return jnp.concatenate([hi, x - hi], axis=0).T.astype(BF16)


def add_slots(plan, first, chunks, size, blocks, pieces, tot):
    @pl.loop(0, chunks)
    def _(c):
        parts = []
        for e in range(CHUNK):
            at = first + c * CHUNK + e
            parts.append((plan[at + size], bdot(blocks[plan[at]], pieces[plan[at + 2 * size]])))
        for row, part in parts:
            tot[row] += part


def put_piece(pieces, at, x):
    bs = x.shape[1]
    t = turned(x)
    pieces[at, :bs] = t
    pieces[at, bs:] = t


def near_kernel(plan, blocks, mid, tot, halves, gram, pieces):
    nbd, bs, _ = tot.shape
    bw = mid.shape[0]
    size = plan.shape[0] // 6
    pieces[nbd] = jnp.zeros((2 * bs, 2 * bw), BF16)
    tot[...] = jnp.zeros_like(tot)

    @pl.loop(0, nbd, unroll=4)
    def _(b):
        put_piece(pieces, b, mid[:, pl.ds(pl.multiple_of(b * bs, bs), bs)])

    @pl.loop(0, blocks.shape[0], unroll=4)
    def _(k):
        halves[k] = jnp.concatenate(split(blocks[k]), axis=1)

    add_slots(plan, 1, plan[0], size, halves, pieces, tot)
    g = jnp.zeros((bw, 2 * bw), F32)
    for b in range(0, nbd, RB):
        hi, lo = split(mid[:, b * bs : (b + RB) * bs])
        w = jnp.concatenate([pieces[b + r, :bs] for r in range(RB)], axis=0)
        g = g + bdot(hi, w) + bdot(lo, w)
    gram[...] = g[:, :bw] + g[:, bw:]


def far_kernel(plan, halves, stored, left, right, near, mid, prev, gram, u_out, m_out, tot, pieces, ut, acc, accw):
    nbd, bs, _ = tot.shape
    bw, n = mid.shape
    ks = stored.shape[0]
    size = plan.shape[0] // 6
    pieces[2 * nbd] = jnp.zeros((2 * bs, 2 * bw), BF16)
    for k, src in enumerate((left, right)):

        @pl.loop(0, nbd, unroll=4)
        def _(b):
            put_piece(pieces, k * nbd + b, src[:, pl.ds(pl.multiple_of(b * bs, bs), bs)])

    tot[...] = jnp.zeros_like(tot)
    add_slots(plan, 3 * size + 1, plan[3 * size], size, halves, pieces, tot)

    @pl.loop(0, nbd, unroll=RB)
    def _(b):
        here = pl.ds(pl.multiple_of(b * bs, bs), bs)
        t = (tot[b] + near[b]).T
        u = t[:bw] + t[bw:]
        u_out[:, here] = u
        ut[here] = turned(u)

    acc[...] = jnp.zeros_like(acc)
    accw[...] = jnp.zeros_like(accw)

    @pl.loop(0, n // TILE)
    def _(b):
        here = pl.ds(pl.multiple_of(b * TILE, TILE), TILE)
        t = ut[here]
        shi, slo = split(stored[:, here])
        acc[...] += bdot(shi, t) + bdot(slo, t)
        rhi, rlo = split(jnp.concatenate([mid[:, here], prev[:, here], u_out[:, here]], axis=0))
        accw[...] += bdot(rhi, t) + bdot(rlo, t)

    t = acc[...].T
    a = t[:bw] + t[bw:]
    m_out[:bw, : ks // 2] = a[:, : ks // 2]
    m_out[bw:, : ks // 2] = a[:, ks // 2 :]
    w = accw[...]
    w = w[:, :bw] + w[:, bw:]
    m_out[:bw, ks // 2 :] = jnp.concatenate([w[:bw], gram[...]], axis=1)
    m_out[bw:, ks // 2 :] = jnp.concatenate([w[bw : 2 * bw], w[2 * bw :]], axis=1)


VMEM = pl.BlockSpec(memory_space=pltpu.VMEM)
SMEM = pl.BlockSpec(memory_space=pltpu.SMEM)


def near_op(plan, blocks, mid, nbd):
    _, bs, _ = blocks.shape
    bw, n = mid.shape
    return pl.pallas_call(
        near_kernel,
        in_specs=[SMEM, VMEM, VMEM],
        out_specs=[VMEM] * 3,
        out_shape=[
            jax.ShapeDtypeStruct((nbd, bs, 2 * bw), F32),
            jax.ShapeDtypeStruct((blocks.shape[0], bs, 2 * bs), BF16),
            jax.ShapeDtypeStruct((bw, bw), F32),
        ],
        scratch_shapes=[pltpu.VMEM((nbd + 1, 2 * bs, 2 * bw), BF16)],
        compiler_params=pltpu.CompilerParams(vmem_limit_bytes=VMEM_LIMIT),
        cost_estimate=pl.CostEstimate(flops=2 * 10**9, bytes_accessed=12 * 2**20, transcendentals=0),
        name="near_op",
    )(plan, blocks, mid)


def far_op(plan, halves, stored, left, right, near, mid, prev, gram):
    nbd, bs, _ = near.shape
    bw, n = mid.shape
    ks = stored.shape[0]
    return pl.pallas_call(
        far_kernel,
        in_specs=[SMEM] + [VMEM] * 8,
        out_specs=[VMEM] * 2,
        scratch_shapes=[
            pltpu.VMEM((nbd, bs, 2 * bw), F32),
            pltpu.VMEM((2 * nbd + 1, 2 * bs, 2 * bw), BF16),
            pltpu.VMEM((n, 2 * bw), BF16),
            pltpu.VMEM((ks, 2 * bw), F32),
            pltpu.VMEM((3 * bw, 2 * bw), F32),
        ],
        out_shape=[
            jax.ShapeDtypeStruct((bw, n), F32),
            jax.ShapeDtypeStruct((2 * bw, ks // 2 + 2 * bw), F32),
        ],
        compiler_params=pltpu.CompilerParams(vmem_limit_bytes=VMEM_LIMIT),
        cost_estimate=pl.CostEstimate(flops=2 * 10**9, bytes_accessed=20 * 2**20, transcendentals=0),
        name="far_op",
    )(plan, halves, stored, left, right, near, mid, prev, gram)


def make_plan(local, used, nbd):
    slots = local.shape[1]
    total_slots = nbd * slots
    size = -(-total_slots // CHUNK) * CHUNK + 1
    local, used = local.reshape(-1), used.reshape(-1)
    mine = (local >= nbd) & (local < 2 * nbd)
    ids = jnp.arange(total_slots, dtype=jnp.int32)
    rows = jnp.arange(size - 1, dtype=jnp.int32)
    out = []
    for flag, piece, empty in (
        (used & mine, local - nbd, nbd),
        (used & ~mine, jnp.where(local < nbd, local, local - nbd), 2 * nbd),
    ):
        before = jnp.sum(((ids[None, :] < ids[:, None]) & flag[None, :]).astype(jnp.int32), axis=1)
        hit = (before[None, :] == rows[:, None]) & flag[None, :]
        count = jnp.sum(flag.astype(jnp.int32))
        slot = jnp.sum(jnp.where(hit, ids[None, :], 0), axis=1)
        where = jnp.sum(jnp.where(hit, piece[None, :], 0), axis=1)
        where = jnp.where(rows < count, where, empty)
        zero = jnp.zeros((1,), jnp.int32)
        chunks = (count + CHUNK - 1) // CHUNK
        out += [chunks[None], slot, zero, slot // slots, zero, where]
    return jnp.concatenate(out)


def project_kernel(cs, cw, stored, *refs):
    arrays, out = refs[:-1], refs[-1]
    bw, n = out.shape
    chi, clo = split(jnp.concatenate([cs[...], cw[...]], axis=1))
    c2 = jnp.concatenate([chi, clo], axis=0)

    @pl.loop(0, n // TILE)
    def _(i):
        here = pl.ds(pl.multiple_of(i * TILE, TILE), TILE)
        dhi, dlo = split(jnp.concatenate([stored[:, here]] + [a[:, here] for a in arrays], axis=0))
        t = bdot(c2, dhi)
        out[:, here] = t[:bw] + t[bw:] + bdot(chi, dlo)


def project(cs, cw, stored, *arrays):
    vmem = pl.BlockSpec(memory_space=pltpu.VMEM)
    return pl.pallas_call(
        project_kernel,
        in_specs=[vmem] * (3 + len(arrays)),
        out_specs=vmem,
        out_shape=jax.ShapeDtypeStruct(arrays[0].shape, F32),
        compiler_params=pltpu.CompilerParams(vmem_limit_bytes=VMEM_LIMIT),
        name="project",
    )(cs, cw, stored, *arrays)


PANEL = 4


def factor_of(gram):
    n = gram.shape[0]
    row = lax.broadcasted_iota(jnp.int32, (n, 2 * n), 0)
    lane = lax.broadcasted_iota(jnp.int32, (n, 2 * n), 1)
    eye = (lane == row + n).astype(F32)
    m = jnp.where(lane < n, jnp.concatenate([gram, gram], axis=1), eye)
    scale = jnp.zeros((n, 2 * n), F32)
    for p in range(0, n, PANEL):
        cols = [jnp.broadcast_to(m[:, p + j : p + j + 1], (n, 2 * n)) for j in range(PANEL)]
        for j in range(PANEL):
            k = p + j
            pivot = cols[j][k : k + 1]
            root = lax.rsqrt(pivot)
            root = root * (1.5 - 0.5 * pivot * root * root)
            f = jnp.where(row > k, cols[j] * (root * root), 0.0)
            scale = jnp.where(row == k, root, scale)
            m = m - f * m[k : k + 1]
            for q in range(j + 1, PANEL):
                cols[q] = cols[q] - f * cols[q][k : k + 1]
    m = m * scale
    upper = jnp.where(lane >= row, m, 0.0)[:, :n]
    return upper, m[:, n:]


def unpacked(t, bw):
    half = t.shape[1] - 2 * bw
    mst = jnp.concatenate([t[:bw, :half], t[bw:, :half]], axis=1)
    a = t[:bw, half:]
    b = t[bw:, half:]
    return mst, a[:, :bw], a[:, bw:], b[:, :bw], b[:, bw:]


def first_kernel(packed, s, c1t_out, minus_dt):
    half = packed.shape[0]
    bw = c1t_out.shape[0]
    s12 = packed[:, half : 2 * half]
    s[:half] = packed[:, : 2 * half]
    s[half:] = jnp.concatenate([s12.T, packed[:, 2 * half : 3 * half]], axis=1)
    t = packed[:, 3 * half :].T
    c1t = jnp.concatenate([t[:bw], t[bw:]], axis=1)
    c1t_out[...] = c1t
    minus_dt[...] = dot_nn(c1t, s[...]) - 2.0 * c1t


def after_first_kernel(s, c1t, minus_dt, c3t):
    c3t[...] = c1t[...] + dot_nn(minus_dt[...], s[...])


def second_kernel(t, s, c3t, cs, cw, keep):
    bw = c3t.shape[0]
    mst, h, g, _, _ = unpacked(t[...], bw)
    _, e1 = factor_of(g)
    k1t = dot_nn(e1, c3t[...])
    c1t = dot_nn(e1, mst)
    c1vt = dot_nt(e1, dot_nn(e1, h))
    c2t = c1t - dot_nn(c1t, s[...]) - dot_nn(c1vt, k1t)
    c2vt = -dot_nt(c1t, k1t)
    dvt = c1vt + c2vt
    cs[...] = -(c1t + c2t)
    cw[...] = jnp.concatenate([e1, -dot_nn(dvt, e1)], axis=1)
    keep[:bw] = k1t
    keep[bw : 2 * bw] = c2t
    keep[2 * bw :, : 4 * bw] = jnp.concatenate([e1, c2vt, dvt.T, dvt], axis=1)


def after_kernel(s, keep, c3):
    bw = c3.shape[0]
    k1t, c2t, c2vt = keep[:bw], keep[bw : 2 * bw], keep[2 * bw :, bw : 2 * bw]
    c3[:, : s.shape[0]] = c2t - dot_nn(c2t, s[...]) - dot_nn(c2vt, k1t)
    c3vt = -dot_nt(c2t, k1t)
    c3[:, s.shape[0] :] = jnp.concatenate([c3vt, c3vt], axis=1)


def third_kernel(t, s, c3, keep, cs, cw, diags, uppers, *, size):
    bw = c3.shape[0]
    sm = s[...]
    k1t, e1 = keep[:bw], keep[2 * bw :, :bw]
    c3st, c3vt = c3[:, : sm.shape[0]], c3[:, sm.shape[0] : sm.shape[0] + bw]
    mst, h, g, h12, uu = unpacked(t[...], bw)
    lt2, e2 = factor_of(g)
    uppers[0] = lt2
    k2t = dot_nn(e2, c3st)
    n12t = dot_nn(e2, c3vt)
    c1t = dot_nn(e2, mst)
    c1at = dot_nt(e2, dot_nn(e2, h))
    c1bt = dot_nt(e2, dot_nn(e1, h12))
    yy = dot_nt(dot_nn(e2, uu), e2)
    dst = 2.0 * c1t - dot_nn(c1t, sm) - dot_nn(c1at, k2t) - dot_nn(c1bt, k1t)
    dat = c1at - dot_nt(c1t, k2t) - dot_nt(c1bt, n12t)
    dbt = c1bt - dot_nt(c1t, k1t) - dot_nn(c1at, n12t)
    diags[0] = keep[2 * bw :, 2 * bw : 3 * bw]
    diags[1] = dat.T
    c3s = c1t - dot_nn(dst, sm) - dot_nn(dat, k2t) - dot_nn(dbt, k1t)
    c3a = c1at - dot_nt(dst, k2t) - dat - dot_nt(dbt, n12t)
    c3b = c1bt - dot_nt(dst, k1t) - dot_nn(dat, n12t) - dbt
    g3 = yy - dot_nt(c1t, dst) - dot_nt(dst, c3s)
    g3 = g3 - dot_nt(c1at, dat) - dot_nt(dat, c3a) - dot_nt(c1bt, dbt) - dot_nt(dbt, c3b)
    lt3, e3 = factor_of(0.5 * (g3 + g3.T))
    uppers[1] = lt3
    e3 = e3 * math.sqrt(size)
    cs[...] = -dot_nn(e3, dst)
    cw[...] = jnp.concatenate(
        [dot_nn(e3, e2), -dot_nn(e3, dot_nn(dat, e2)), -dot_nn(e3, dot_nn(dbt, e1))], axis=1
    )


def small(kernel, name, shapes, *args, flops=10**10):
    return pl.pallas_call(
        kernel,
        out_shape=[jax.ShapeDtypeStruct(s, F32) for s in shapes],
        compiler_params=pltpu.CompilerParams(vmem_limit_bytes=VMEM_LIMIT),
        cost_estimate=pl.CostEstimate(flops=flops, bytes_accessed=2 * 2**20, transcendentals=0),
        name=name,
    )(*args)


def on_device(blocks, pattern, counts, stored, start_block):
    nbd, slots, bs, _ = blocks.shape
    bw, n = start_block.shape
    ks = stored.shape[0]
    half = ks // 2
    devices = lax.axis_size(AXES)
    position = lax.axis_index(AXES)
    nb = nbd * devices
    local = (pattern - (position - 1) * nbd) % nb
    used = jnp.arange(slots, dtype=jnp.int32)[None, :] < counts[:, None]
    plan = make_plan(local, used, nbd)
    tiles = blocks.reshape(nbd * slots, bs, bs)
    up = [(i, (i + 1) % devices) for i in range(devices)]
    down = [(j, i) for i, j in up]

    def halo(w):
        return lax.ppermute(w, AXES, up), lax.ppermute(w, AXES, down)

    top = dot_nt(stored[:half], stored, HIGH)
    corner = dot_nt(stored[half:], stored[half:], HIGH)
    first = dot_nt(stored, start_block, HIGH)
    packed = total(jnp.concatenate([top, corner, first[:half], first[half:]], axis=1))
    wide = (bw, ks)
    s, c1t, minus_dt = small(first_kernel, "first", [(ks, ks), wide, wide], packed)
    w1 = project(minus_dt, jnp.eye(bw, dtype=F32), stored, start_block)
    (c3t,) = small(after_first_kernel, "after_first", [wide], s, c1t, minus_dt, flops=10**8)

    def apply(w, prev):
        left, right = halo(w)
        near, halves, gram = near_op(plan, tiles, w, nbd)
        return far_op(plan, halves, stored, left, right, near, w, prev, gram)

    u1, m1 = apply(w1, w1)
    cs, cw, keep = small(second_kernel, "second", [wide, (bw, 2 * bw), (3 * bw, ks)], total(m1), s, c3t)
    w2 = project(cs, cw, stored, u1, w1)
    (c3,) = small(after_kernel, "after", [(bw, ks + 2 * bw)], s, keep, flops=10**8)

    u2, m2 = apply(w2, w1)
    cs, cw, diags, uppers = small(
        functools.partial(third_kernel, size=nb * bs),
        "third",
        [wide, (bw, 3 * bw), (2, bw, bw), (2, bw, bw)],
        total(m2), s, c3, keep,
    )
    return diags, uppers, project(cs, cw, stored, u2, w2, w1)


def solution(mesh):
    in_specs = (
        P(AXES, None, None, None),
        P(AXES, None),
        P(AXES),
        P(None, AXES),
        P(None, AXES),
    )
    out_specs = (P(), P(), P(None, AXES))
    return jax.shard_map(on_device, mesh=mesh, in_specs=in_specs, out_specs=out_specs, check_vma=False)
```

```python
import functools
import math

import jax
import jax.numpy as jnp
from jax import lax
from jax.experimental import pallas as pl
from jax.experimental.pallas import tpu as pltpu
from jax.sharding import PartitionSpec as P

AXES = ("row", "basis", "rep")
HIGH = lax.Precision.HIGH
FULL = lax.Precision.HIGHEST
F32 = jnp.float32
BF16 = jnp.bfloat16
RB = 4
CHUNK = 4
TILE = 512
VMEM_LIMIT = 12 * 1024 * 1024


def dot_nt(a, b, precision=FULL):
    return lax.dot_general(a, b, (((1,), (1,)), ((), ())), precision=precision, preferred_element_type=F32)


def dot_tn(a, b, precision=FULL):
    return lax.dot_general(a, b, (((0,), (0,)), ((), ())), precision=precision, preferred_element_type=F32)


def dot_nn(a, b, precision=FULL):
    return lax.dot_general(a, b, (((1,), (0,)), ((), ())), precision=precision, preferred_element_type=F32)


def bdot(a, b):
    return jnp.dot(a, b, preferred_element_type=F32)


def total(x):
    parts = lax.all_to_all(x, AXES, 0, 0, tiled=True)
    mine = jnp.sum(parts, axis=0, keepdims=True)
    return lax.all_to_all(jnp.broadcast_to(mine, x.shape), AXES, 0, 0, tiled=True)[:, 0]


def split(x):
    hi = x.astype(BF16)
    lo = (x - hi.astype(F32)).astype(BF16)
    return hi, lo


def stacked(x):
    return jnp.concatenate(split(x), axis=0)


def bdot_nt(a, b):
    return lax.dot_general(a, b, (((1,), (1,)), ((), ())), preferred_element_type=F32)


def add_slots(plan, first, chunks, size, halves, pieces, tot):
    @pl.loop(0, chunks)
    def _(c):
        parts = []
        for e in range(CHUNK):
            at = first + c * CHUNK + e
            v = pieces[plan[at + 2 * size]]
            parts.append((plan[at + size], bdot_nt(jnp.concatenate([v, v], axis=1), halves[plan[at]])))
        for row, part in parts:
            tot[row] += part


def near_kernel(plan, blocks, mid, tot, halves, gram, pieces):
    nbd, _, bs = tot.shape
    bw, n = mid.shape
    size = plan.shape[0] // 6
    pieces[nbd] = jnp.zeros((2 * bw, bs), BF16)
    tot[...] = jnp.zeros_like(tot)

    @pl.loop(0, nbd, unroll=4)
    def _(b):
        pieces[b] = stacked(mid[:, pl.ds(pl.multiple_of(b * bs, bs), bs)])

    @pl.loop(0, blocks.shape[0], unroll=4)
    def _(k):
        halves[k] = jnp.concatenate(split(blocks[k]), axis=1)

    add_slots(plan, 1, plan[0], size, halves, pieces, tot)
    g = jnp.zeros((bw, 2 * bw), F32)
    for b in range(0, n, TILE):
        hi, lo = split(mid[:, b : b + TILE])
        w = jnp.concatenate([hi, lo], axis=0)
        g = g + bdot_nt(hi, w) + bdot_nt(lo, w)
    gram[...] = g[:, :bw] + g[:, bw:]


def far_kernel(plan, halves, stored, left, right, near, mid, prev, gram, u_out, m_out, tot, pieces, acc, accw):
    nbd, _, bs = tot.shape
    bw, n = mid.shape
    ks = stored.shape[0]
    size = plan.shape[0] // 6
    pieces[2 * nbd] = jnp.zeros((2 * bw, bs), BF16)
    for k, src in enumerate((left, right)):

        @pl.loop(0, nbd, unroll=4)
        def _(b):
            pieces[k * nbd + b] = stacked(src[:, pl.ds(pl.multiple_of(b * bs, bs), bs)])

    tot[...] = jnp.zeros_like(tot)
    add_slots(plan, 3 * size + 1, plan[3 * size], size, halves, pieces, tot)
    acc[...] = jnp.zeros_like(acc)
    accw[...] = jnp.zeros_like(accw)
    per = TILE // bs

    @pl.loop(0, n // TILE)
    def _(b):
        here = pl.ds(pl.multiple_of(b * TILE, TILE), TILE)
        us = []
        for r in range(per):
            t = tot[b * per + r] + near[b * per + r]
            us.append(t[:bw] + t[bw:])
        u = jnp.concatenate(us, axis=1)
        u_out[:, here] = u
        u2 = stacked(u)
        shi, slo = split(stored[:, here])
        acc[...] += bdot_nt(shi, u2) + bdot_nt(slo, u2)
        rhi, rlo = split(jnp.concatenate([mid[:, here], prev[:, here], u], axis=0))
        accw[...] += bdot_nt(rhi, u2) + bdot_nt(rlo, u2)

    t = acc[...].T
    a = t[:bw] + t[bw:]
    m_out[:bw, 0, : ks // 2] = a[:, : ks // 2]
    m_out[bw:, 0, : ks // 2] = a[:, ks // 2 :]
    w = accw[...]
    w = w[:, :bw] + w[:, bw:]
    m_out[:bw, 0, ks // 2 :] = jnp.concatenate([w[:bw], gram[...]], axis=1)
    m_out[bw:, 0, ks // 2 :] = jnp.concatenate([w[bw : 2 * bw], w[2 * bw :]], axis=1)


VMEM = pl.BlockSpec(memory_space=pltpu.VMEM)
SMEM = pl.BlockSpec(memory_space=pltpu.SMEM)


def near_op(plan, blocks, mid, nbd):
    _, bs, _ = blocks.shape
    bw, n = mid.shape
    return pl.pallas_call(
        near_kernel,
        in_specs=[SMEM, VMEM, VMEM],
        out_specs=[VMEM] * 3,
        out_shape=[
            jax.ShapeDtypeStruct((nbd, 2 * bw, bs), F32),
            jax.ShapeDtypeStruct((blocks.shape[0], bs, 2 * bs), BF16),
            jax.ShapeDtypeStruct((bw, bw), F32),
        ],
        scratch_shapes=[pltpu.VMEM((nbd + 1, 2 * bw, bs), BF16)],
        compiler_params=pltpu.CompilerParams(vmem_limit_bytes=VMEM_LIMIT),
        cost_estimate=pl.CostEstimate(flops=2 * 10**9, bytes_accessed=12 * 2**20, transcendentals=0),
        name="near_op",
    )(plan, blocks, mid)


def far_op(plan, halves, stored, left, right, near, mid, prev, gram):
    nbd, _, bs = near.shape
    bw, n = mid.shape
    ks = stored.shape[0]
    return pl.pallas_call(
        far_kernel,
        in_specs=[SMEM] + [VMEM] * 8,
        out_specs=[VMEM] * 2,
        scratch_shapes=[
            pltpu.VMEM((nbd, 2 * bw, bs), F32),
            pltpu.VMEM((2 * nbd + 1, 2 * bw, bs), BF16),
            pltpu.VMEM((ks, 2 * bw), F32),
            pltpu.VMEM((3 * bw, 2 * bw), F32),
        ],
        out_shape=[
            jax.ShapeDtypeStruct((bw, n), F32),
            jax.ShapeDtypeStruct((2 * bw, 1, ks // 2 + 2 * bw), F32),
        ],
        compiler_params=pltpu.CompilerParams(vmem_limit_bytes=VMEM_LIMIT),
        cost_estimate=pl.CostEstimate(flops=2 * 10**9, bytes_accessed=20 * 2**20, transcendentals=0),
        name="far_op",
    )(plan, halves, stored, left, right, near, mid, prev, gram)


def make_plan(local, used, nbd):
    slots = local.shape[1]
    total_slots = nbd * slots
    size = -(-total_slots // CHUNK) * CHUNK + 1
    local, used = local.reshape(-1), used.reshape(-1)
    mine = (local >= nbd) & (local < 2 * nbd)
    ids = jnp.arange(total_slots, dtype=jnp.int32)
    rows = jnp.arange(size - 1, dtype=jnp.int32)
    out = []
    for flag, piece, empty in (
        (used & mine, local - nbd, nbd),
        (used & ~mine, jnp.where(local < nbd, local, local - nbd), 2 * nbd),
    ):
        before = jnp.sum(((ids[None, :] < ids[:, None]) & flag[None, :]).astype(jnp.int32), axis=1)
        hit = (before[None, :] == rows[:, None]) & flag[None, :]
        count = jnp.sum(flag.astype(jnp.int32))
        slot = jnp.sum(jnp.where(hit, ids[None, :], 0), axis=1)
        where = jnp.sum(jnp.where(hit, piece[None, :], 0), axis=1)
        where = jnp.where(rows < count, where, empty)
        zero = jnp.zeros((1,), jnp.int32)
        chunks = (count + CHUNK - 1) // CHUNK
        out += [chunks[None], slot, zero, slot // slots, zero, where]
    return jnp.concatenate(out)


def project_kernel(cs, cw, stored, *refs):
    arrays, out = refs[:-1], refs[-1]
    bw, n = out.shape
    chi, clo = split(jnp.concatenate([cs[...], cw[...]], axis=1))
    c2 = jnp.concatenate([chi, clo], axis=0)

    @pl.loop(0, n // TILE)
    def _(i):
        here = pl.ds(pl.multiple_of(i * TILE, TILE), TILE)
        dhi, dlo = split(jnp.concatenate([stored[:, here]] + [a[:, here] for a in arrays], axis=0))
        t = bdot(c2, dhi)
        out[:, here] = t[:bw] + t[bw:] + bdot(chi, dlo)


def project(cs, cw, stored, *arrays):
    vmem = pl.BlockSpec(memory_space=pltpu.VMEM)
    return pl.pallas_call(
        project_kernel,
        in_specs=[vmem] * (3 + len(arrays)),
        out_specs=vmem,
        out_shape=jax.ShapeDtypeStruct(arrays[0].shape, F32),
        compiler_params=pltpu.CompilerParams(vmem_limit_bytes=VMEM_LIMIT),
        name="project",
    )(cs, cw, stored, *arrays)


PANEL = 4


def factor_of(gram):
    n = gram.shape[0]
    row = lax.broadcasted_iota(jnp.int32, (n, 2 * n), 0)
    lane = lax.broadcasted_iota(jnp.int32, (n, 2 * n), 1)
    eye = (lane == row + n).astype(F32)
    m = jnp.where(lane < n, jnp.concatenate([gram, gram], axis=1), eye)
    scale = jnp.zeros((n, 2 * n), F32)
    for p in range(0, n, PANEL):
        cols = [jnp.broadcast_to(m[:, p + j : p + j + 1], (n, 2 * n)) for j in range(PANEL)]
        for j in range(PANEL):
            k = p + j
            pivot = cols[j][k : k + 1]
            root = lax.rsqrt(pivot)
            root = root * (1.5 - 0.5 * pivot * root * root)
            f = jnp.where(row > k, cols[j] * (root * root), 0.0)
            scale = jnp.where(row == k, root, scale)
            m = m - f * m[k : k + 1]
            for q in range(j + 1, PANEL):
                cols[q] = cols[q] - f * cols[q][k : k + 1]
    m = m * scale
    upper = jnp.where(lane >= row, m, 0.0)[:, :n]
    return upper, m[:, n:]


def unpacked(t, bw):
    half = t.shape[1] - 2 * bw
    mst = jnp.concatenate([t[:bw, :half], t[bw:, :half]], axis=1)
    a = t[:bw, half:]
    b = t[bw:, half:]
    return mst, a[:, :bw], a[:, bw:], b[:, :bw], b[:, bw:]


def first_kernel(t, s, c1t_out, minus_dt):
    bw, ks = c1t_out.shape
    half = ks // 2
    packed = t[...]
    cut = packed.shape[1] // 2
    packed = jnp.concatenate([packed[:, :cut], packed[:, cut:]], axis=0)
    s12 = packed[:, half : 2 * half]
    s[:half] = packed[:, : 2 * half]
    s[half:] = jnp.concatenate([s12.T, packed[:, 2 * half : 3 * half]], axis=1)
    t = packed[:, 3 * half :].T
    c1t = jnp.concatenate([t[:bw], t[bw:]], axis=1)
    c1t_out[...] = c1t
    minus_dt[...] = dot_nn(c1t, s[...]) - 2.0 * c1t


def after_first_kernel(s, c1t, minus_dt, c3t):
    c3t[...] = c1t[...] + dot_nn(minus_dt[...], s[...])


def second_kernel(t, s, c3t, cs, cw, keep):
    bw = c3t.shape[0]
    mst, h, g, _, _ = unpacked(t[...], bw)
    _, e1 = factor_of(g)
    k1t = dot_nn(e1, c3t[...])
    c1t = dot_nn(e1, mst)
    c1vt = dot_nt(e1, dot_nn(e1, h))
    c2t = c1t - dot_nn(c1t, s[...]) - dot_nn(c1vt, k1t)
    c2vt = -dot_nt(c1t, k1t)
    dvt = c1vt + c2vt
    cs[...] = -(c1t + c2t)
    cw[...] = jnp.concatenate([e1, -dot_nn(dvt, e1)], axis=1)
    keep[:bw] = k1t
    keep[bw : 2 * bw] = c2t
    keep[2 * bw :, : 4 * bw] = jnp.concatenate([e1, c2vt, dvt.T, dvt], axis=1)


def after_kernel(s, keep, c3):
    bw = c3.shape[0]
    k1t, c2t, c2vt = keep[:bw], keep[bw : 2 * bw], keep[2 * bw :, bw : 2 * bw]
    c3[:, : s.shape[0]] = c2t - dot_nn(c2t, s[...]) - dot_nn(c2vt, k1t)
    c3vt = -dot_nt(c2t, k1t)
    c3[:, s.shape[0] :] = jnp.concatenate([c3vt, c3vt], axis=1)


def third_kernel(t, s, c3, keep, cs, cw, diags, uppers, *, size):
    bw = c3.shape[0]
    sm = s[...]
    k1t, e1 = keep[:bw], keep[2 * bw :, :bw]
    c3st, c3vt = c3[:, : sm.shape[0]], c3[:, sm.shape[0] : sm.shape[0] + bw]
    mst, h, g, h12, uu = unpacked(t[...], bw)
    lt2, e2 = factor_of(g)
    uppers[0] = lt2
    k2t = dot_nn(e2, c3st)
    n12t = dot_nn(e2, c3vt)
    c1t = dot_nn(e2, mst)
    c1at = dot_nt(e2, dot_nn(e2, h))
    c1bt = dot_nt(e2, dot_nn(e1, h12))
    yy = dot_nt(dot_nn(e2, uu), e2)
    dst = 2.0 * c1t - dot_nn(c1t, sm) - dot_nn(c1at, k2t) - dot_nn(c1bt, k1t)
    dat = c1at - dot_nt(c1t, k2t) - dot_nt(c1bt, n12t)
    dbt = c1bt - dot_nt(c1t, k1t) - dot_nn(c1at, n12t)
    diags[0] = keep[2 * bw :, 2 * bw : 3 * bw]
    diags[1] = dat.T
    c3s = c1t - dot_nn(dst, sm) - dot_nn(dat, k2t) - dot_nn(dbt, k1t)
    c3a = c1at - dot_nt(dst, k2t) - dat - dot_nt(dbt, n12t)
    c3b = c1bt - dot_nt(dst, k1t) - dot_nn(dat, n12t) - dbt
    g3 = yy - dot_nt(c1t, dst) - dot_nt(dst, c3s)
    g3 = g3 - dot_nt(c1at, dat) - dot_nt(dat, c3a) - dot_nt(c1bt, dbt) - dot_nt(dbt, c3b)
    lt3, e3 = factor_of(0.5 * (g3 + g3.T))
    uppers[1] = lt3
    e3 = e3 * math.sqrt(size)
    cs[...] = -dot_nn(e3, dst)
    cw[...] = jnp.concatenate(
        [dot_nn(e3, e2), -dot_nn(e3, dot_nn(dat, e2)), -dot_nn(e3, dot_nn(dbt, e1))], axis=1
    )


def small(kernel, name, shapes, *args, flops=10**10):
    return pl.pallas_call(
        kernel,
        out_shape=[jax.ShapeDtypeStruct(s, F32) for s in shapes],
        compiler_params=pltpu.CompilerParams(vmem_limit_bytes=VMEM_LIMIT),
        cost_estimate=pl.CostEstimate(flops=flops, bytes_accessed=2 * 2**20, transcendentals=0),
        name=name,
    )(*args)


def on_device(blocks, pattern, counts, stored, start_block):
    nbd, slots, bs, _ = blocks.shape
    bw, n = start_block.shape
    ks = stored.shape[0]
    devices = lax.axis_size(AXES)
    position = lax.axis_index(AXES)
    nb = nbd * devices
    local = (pattern - (position - 1) * nbd) % nb
    used = jnp.arange(slots, dtype=jnp.int32)[None, :] < counts[:, None]
    plan = make_plan(local, used, nbd)
    tiles = blocks.reshape(nbd * slots, bs, bs)
    up = [(i, (i + 1) % devices) for i in range(devices)]
    down = [(j, i) for i, j in up]

    def halo(w):
        return lax.ppermute(w, AXES, up), lax.ppermute(w, AXES, down)

    half = ks // 2
    top = dot_nt(stored[:half], stored, HIGH)
    corner = dot_nt(stored[half:], stored[half:], HIGH)
    first = dot_nt(stored, start_block, HIGH)
    packed = jnp.concatenate([top, corner, first[:half], first[half:]], axis=1)
    packed = jnp.concatenate([packed[:devices], packed[devices:]], axis=1)
    packed = total(packed[:, None, :])
    wide = (bw, ks)
    s, c1t, minus_dt = small(first_kernel, "first", [(ks, ks), wide, wide], packed)
    w1 = project(minus_dt, jnp.eye(bw, dtype=F32), stored, start_block)
    (c3t,) = small(after_first_kernel, "after_first", [wide], s, c1t, minus_dt, flops=10**8)

    def apply(w, prev):
        left, right = halo(w)
        near, halves, gram = near_op(plan, tiles, w, nbd)
        return far_op(plan, halves, stored, left, right, near, w, prev, gram)

    u1, m1 = apply(w1, w1)
    cs, cw, keep = small(second_kernel, "second", [wide, (bw, 2 * bw), (3 * bw, ks)], total(m1), s, c3t)
    w2 = project(cs, cw, stored, u1, w1)
    (c3,) = small(after_kernel, "after", [(bw, ks + 2 * bw)], s, keep, flops=10**8)

    u2, m2 = apply(w2, w1)
    cs, cw, diags, uppers = small(
        functools.partial(third_kernel, size=nb * bs),
        "third",
        [wide, (bw, 3 * bw), (2, bw, bw), (2, bw, bw)],
        total(m2), s, c3, keep,
    )
    return diags, uppers, project(cs, cw, stored, u2, w2, w1)


def solution(mesh):
    in_specs = (
        P(AXES, None, None, None),
        P(AXES, None),
        P(AXES),
        P(None, AXES),
        P(None, AXES),
    )
    out_specs = (P(), P(), P(None, AXES))
    return jax.shard_map(on_device, mesh=mesh, in_specs=in_specs, out_specs=out_specs, check_vma=False)
```

```python
import functools
import math

import jax
import jax.numpy as jnp
from jax import lax
from jax.experimental import pallas as pl
from jax.experimental.pallas import tpu as pltpu
from jax.sharding import PartitionSpec as P

AXES = ("row", "basis", "rep")
HIGH = lax.Precision.HIGH
FULL = lax.Precision.HIGHEST
F32 = jnp.float32
BF16 = jnp.bfloat16
RB = 4
CHUNK = 8
TILE = 1024
VMEM_LIMIT = 12 * 1024 * 1024


def dot_nt(a, b, precision=FULL):
    return lax.dot_general(a, b, (((1,), (1,)), ((), ())), precision=precision, preferred_element_type=F32)


def dot_tn(a, b, precision=FULL):
    return lax.dot_general(a, b, (((0,), (0,)), ((), ())), precision=precision, preferred_element_type=F32)


def dot_nn(a, b, precision=FULL):
    return lax.dot_general(a, b, (((1,), (0,)), ((), ())), precision=precision, preferred_element_type=F32)


def bdot(a, b):
    return jnp.dot(a, b, preferred_element_type=F32)


def total(x):
    parts = lax.all_to_all(x, AXES, 0, 0, tiled=True)
    mine = jnp.sum(parts, axis=0, keepdims=True)
    return lax.all_to_all(jnp.broadcast_to(mine, x.shape), AXES, 0, 0, tiled=True)[:, 0]


def split(x):
    hi = x.astype(BF16)
    lo = (x - hi.astype(F32)).astype(BF16)
    return hi, lo


def stacked(x):
    return jnp.concatenate(split(x), axis=0)


def bdot_nt(a, b):
    return lax.dot_general(a, b, (((1,), (1,)), ((), ())), preferred_element_type=F32)


def add_slots(plan, first, chunks, size, halves, pieces, tot):
    @pl.loop(0, chunks)
    def _(c):
        parts = []
        for e in range(CHUNK):
            at = first + c * CHUNK + e
            v = pieces[plan[at + 2 * size]]
            parts.append((plan[at + size], bdot_nt(jnp.concatenate([v, v], axis=1), halves[plan[at]])))
        for row, part in parts:
            tot[row] += part


def near_kernel(plan, blocks, mid, tot, halves, gram, pieces):
    nbd, _, bs = tot.shape
    bw, n = mid.shape
    size = plan.shape[0] // 6
    pieces[nbd] = jnp.zeros((2 * bw, bs), BF16)
    tot[...] = jnp.zeros_like(tot)

    @pl.loop(0, nbd, unroll=4)
    def _(b):
        pieces[b] = stacked(mid[:, pl.ds(pl.multiple_of(b * bs, bs), bs)])

    @pl.loop(0, blocks.shape[0], unroll=4)
    def _(k):
        halves[k] = jnp.concatenate(split(blocks[k]), axis=1)

    add_slots(plan, 1, plan[0], size, halves, pieces, tot)
    g = jnp.zeros((bw, 2 * bw), F32)
    for b in range(0, n, TILE):
        hi, lo = split(mid[:, b : b + TILE])
        w = jnp.concatenate([hi, lo], axis=0)
        g = g + bdot_nt(hi, w) + bdot_nt(lo, w)
    gram[...] = g[:, :bw] + g[:, bw:]


def far_kernel(plan, halves, stored, left, right, near, mid, prev, gram, u_out, m_out, tot, pieces, acc, accw):
    nbd, _, bs = tot.shape
    bw, n = mid.shape
    ks = stored.shape[0]
    size = plan.shape[0] // 6
    pieces[2 * nbd] = jnp.zeros((2 * bw, bs), BF16)
    for k, src in enumerate((left, right)):

        @pl.loop(0, nbd, unroll=4)
        def _(b):
            pieces[k * nbd + b] = stacked(src[:, pl.ds(pl.multiple_of(b * bs, bs), bs)])

    tot[...] = jnp.zeros_like(tot)
    add_slots(plan, 3 * size + 1, plan[3 * size], size, halves, pieces, tot)
    acc[...] = jnp.zeros_like(acc)
    accw[...] = jnp.zeros_like(accw)
    per = TILE // bs

    @pl.loop(0, n // TILE)
    def _(b):
        here = pl.ds(pl.multiple_of(b * TILE, TILE), TILE)
        us = []
        for r in range(per):
            t = tot[b * per + r] + near[b * per + r]
            us.append(t[:bw] + t[bw:])
        u = jnp.concatenate(us, axis=1)
        u_out[:, here] = u
        u2 = stacked(u)
        shi, slo = split(stored[:, here])
        acc[...] += bdot_nt(shi, u2) + bdot_nt(slo, u2)
        rhi, rlo = split(jnp.concatenate([mid[:, here], prev[:, here], u], axis=0))
        accw[...] += bdot_nt(rhi, u2) + bdot_nt(rlo, u2)

    t = acc[...].T
    a = t[:bw] + t[bw:]
    m_out[:bw, 0, : ks // 2] = a[:, : ks // 2]
    m_out[bw:, 0, : ks // 2] = a[:, ks // 2 :]
    w = accw[...]
    w = w[:, :bw] + w[:, bw:]
    m_out[:bw, 0, ks // 2 :] = jnp.concatenate([w[:bw], gram[...]], axis=1)
    m_out[bw:, 0, ks // 2 :] = jnp.concatenate([w[bw : 2 * bw], w[2 * bw :]], axis=1)


VMEM = pl.BlockSpec(memory_space=pltpu.VMEM)
SMEM = pl.BlockSpec(memory_space=pltpu.SMEM)


def near_op(plan, blocks, mid, nbd):
    _, bs, _ = blocks.shape
    bw, n = mid.shape
    return pl.pallas_call(
        near_kernel,
        in_specs=[SMEM, VMEM, VMEM],
        out_specs=[VMEM] * 3,
        out_shape=[
            jax.ShapeDtypeStruct((nbd, 2 * bw, bs), F32),
            jax.ShapeDtypeStruct((blocks.shape[0], bs, 2 * bs), BF16),
            jax.ShapeDtypeStruct((bw, bw), F32),
        ],
        scratch_shapes=[pltpu.VMEM((nbd + 1, 2 * bw, bs), BF16)],
        compiler_params=pltpu.CompilerParams(vmem_limit_bytes=VMEM_LIMIT),
        cost_estimate=pl.CostEstimate(flops=2 * 10**9, bytes_accessed=12 * 2**20, transcendentals=0),
        name="near_op",
    )(plan, blocks, mid)


def far_op(plan, halves, stored, left, right, near, mid, prev, gram):
    nbd, _, bs = near.shape
    bw, n = mid.shape
    ks = stored.shape[0]
    return pl.pallas_call(
        far_kernel,
        in_specs=[SMEM] + [VMEM] * 8,
        out_specs=[VMEM] * 2,
        scratch_shapes=[
            pltpu.VMEM((nbd, 2 * bw, bs), F32),
            pltpu.VMEM((2 * nbd + 1, 2 * bw, bs), BF16),
            pltpu.VMEM((ks, 2 * bw), F32),
            pltpu.VMEM((3 * bw, 2 * bw), F32),
        ],
        out_shape=[
            jax.ShapeDtypeStruct((bw, n), F32),
            jax.ShapeDtypeStruct((2 * bw, 1, ks // 2 + 2 * bw), F32),
        ],
        compiler_params=pltpu.CompilerParams(vmem_limit_bytes=VMEM_LIMIT),
        cost_estimate=pl.CostEstimate(flops=2 * 10**9, bytes_accessed=20 * 2**20, transcendentals=0),
        name="far_op",
    )(plan, halves, stored, left, right, near, mid, prev, gram)


def make_plan(local, used, nbd):
    slots = local.shape[1]
    total_slots = nbd * slots
    size = -(-total_slots // CHUNK) * CHUNK + 1
    local, used = local.reshape(-1), used.reshape(-1)
    mine = (local >= nbd) & (local < 2 * nbd)
    ids = jnp.arange(total_slots, dtype=jnp.int32)
    rows = jnp.arange(size - 1, dtype=jnp.int32)
    out = []
    for flag, piece, empty in (
        (used & mine, local - nbd, nbd),
        (used & ~mine, jnp.where(local < nbd, local, local - nbd), 2 * nbd),
    ):
        before = jnp.sum(((ids[None, :] < ids[:, None]) & flag[None, :]).astype(jnp.int32), axis=1)
        hit = (before[None, :] == rows[:, None]) & flag[None, :]
        count = jnp.sum(flag.astype(jnp.int32))
        slot = jnp.sum(jnp.where(hit, ids[None, :], 0), axis=1)
        where = jnp.sum(jnp.where(hit, piece[None, :], 0), axis=1)
        where = jnp.where(rows < count, where, empty)
        zero = jnp.zeros((1,), jnp.int32)
        chunks = (count + CHUNK - 1) // CHUNK
        out += [chunks[None], slot, zero, slot // slots, zero, where]
    return jnp.concatenate(out)


def project_kernel(cs, cw, stored, *refs):
    arrays, out = refs[:-1], refs[-1]
    bw, n = out.shape
    chi, clo = split(jnp.concatenate([cs[...], cw[...]], axis=1))
    c2 = jnp.concatenate([chi, clo], axis=0)

    @pl.loop(0, n // TILE)
    def _(i):
        here = pl.ds(pl.multiple_of(i * TILE, TILE), TILE)
        dhi, dlo = split(jnp.concatenate([stored[:, here]] + [a[:, here] for a in arrays], axis=0))
        t = bdot(c2, dhi)
        out[:, here] = t[:bw] + t[bw:] + bdot(chi, dlo)


def project(cs, cw, stored, *arrays):
    vmem = pl.BlockSpec(memory_space=pltpu.VMEM)
    return pl.pallas_call(
        project_kernel,
        in_specs=[vmem] * (3 + len(arrays)),
        out_specs=vmem,
        out_shape=jax.ShapeDtypeStruct(arrays[0].shape, F32),
        compiler_params=pltpu.CompilerParams(vmem_limit_bytes=VMEM_LIMIT),
        name="project",
    )(cs, cw, stored, *arrays)


PANEL = 4


def factor_of(gram):
    n = gram.shape[0]
    row = lax.broadcasted_iota(jnp.int32, (n, 2 * n), 0)
    lane = lax.broadcasted_iota(jnp.int32, (n, 2 * n), 1)
    eye = (lane == row + n).astype(F32)
    m = jnp.where(lane < n, jnp.concatenate([gram, gram], axis=1), eye)
    pivots = jnp.ones((n, 2 * n), F32)
    for p in range(0, n, PANEL):
        cols = [jnp.broadcast_to(m[:, p + j : p + j + 1], (n, 2 * n)) for j in range(PANEL)]
        for j in range(PANEL):
            k = p + j
            pivot = cols[j][k : k + 1]
            inv = pl.reciprocal(pivot, approx=True)
            inv = inv * (2.0 - pivot * inv)
            inv = inv * (2.0 - pivot * inv)
            pivots = jnp.where(row == k, pivot, pivots)
            f = jnp.where(row > k, cols[j], 0.0) * inv
            for q in range(j + 1, PANEL):
                cols[q] = cols[q] - f * cols[q][k : k + 1]
            m = m - f * m[k : k + 1]
    root = lax.rsqrt(pivots)
    m = m * (root * (1.5 - 0.5 * pivots * root * root))
    upper = jnp.where(lane >= row, m, 0.0)[:, :n]
    return upper, m[:, n:]


def unpacked(t, bw):
    half = t.shape[1] - 2 * bw
    mst = jnp.concatenate([t[:bw, :half], t[bw:, :half]], axis=1)
    a = t[:bw, half:]
    b = t[bw:, half:]
    return mst, a[:, :bw], a[:, bw:], b[:, :bw], b[:, bw:]


def first_kernel(packed, s, c1t_out, minus_dt):
    bw, ks = c1t_out.shape
    cut = ks // 4
    at = 0
    for q in range(4):
        for k in range(q, 4):
            block = packed[:, at : at + cut]
            at += cut
            s[q * cut : (q + 1) * cut, k * cut : (k + 1) * cut] = block
            if k > q:
                s[k * cut : (k + 1) * cut, q * cut : (q + 1) * cut] = block.T
    t = packed[:, at:].T
    c1t = jnp.concatenate([t[q * bw : (q + 1) * bw] for q in range(4)], axis=1)
    c1t_out[...] = c1t
    minus_dt[...] = dot_nn(c1t, s[...]) - 2.0 * c1t


def after_first_kernel(s, c1t, minus_dt, c3t):
    c3t[...] = c1t[...] + dot_nn(minus_dt[...], s[...])


def second_kernel(t, s, c3t, cs, cw, keep):
    bw = c3t.shape[0]
    mst, h, g, _, _ = unpacked(t[...], bw)
    _, e1 = factor_of(g)
    k1t = dot_nn(e1, c3t[...])
    c1t = dot_nn(e1, mst)
    c1vt = dot_nt(e1, dot_nn(e1, h))
    c2t = c1t - dot_nn(c1t, s[...]) - dot_nn(c1vt, k1t)
    c2vt = -dot_nt(c1t, k1t)
    dvt = c1vt + c2vt
    cs[...] = -(c1t + c2t)
    cw[...] = jnp.concatenate([e1, -dot_nn(dvt, e1)], axis=1)
    keep[:bw] = k1t
    keep[bw : 2 * bw] = c2t
    keep[2 * bw :, : 4 * bw] = jnp.concatenate([e1, c2vt, dvt.T, dvt], axis=1)


def after_kernel(s, keep, c3):
    bw = c3.shape[0]
    k1t, c2t, c2vt = keep[:bw], keep[bw : 2 * bw], keep[2 * bw :, bw : 2 * bw]
    c3[:, : s.shape[0]] = c2t - dot_nn(c2t, s[...]) - dot_nn(c2vt, k1t)
    c3vt = -dot_nt(c2t, k1t)
    c3[:, s.shape[0] :] = jnp.concatenate([c3vt, c3vt], axis=1)


def third_kernel(t, s, c3, keep, cs, cw, diags, uppers, *, size):
    bw = c3.shape[0]
    sm = s[...]
    k1t, e1 = keep[:bw], keep[2 * bw :, :bw]
    c3st, c3vt = c3[:, : sm.shape[0]], c3[:, sm.shape[0] : sm.shape[0] + bw]
    mst, h, g, h12, uu = unpacked(t[...], bw)
    lt2, e2 = factor_of(g)
    uppers[0] = lt2
    k2t = dot_nn(e2, c3st)
    n12t = dot_nn(e2, c3vt)
    c1t = dot_nn(e2, mst)
    c1at = dot_nt(e2, dot_nn(e2, h))
    c1bt = dot_nt(e2, dot_nn(e1, h12))
    yy = dot_nt(dot_nn(e2, uu), e2)
    dst = 2.0 * c1t - dot_nn(c1t, sm) - dot_nn(c1at, k2t) - dot_nn(c1bt, k1t)
    dat = c1at - dot_nt(c1t, k2t) - dot_nt(c1bt, n12t)
    dbt = c1bt - dot_nt(c1t, k1t) - dot_nn(c1at, n12t)
    diags[0] = keep[2 * bw :, 2 * bw : 3 * bw]
    diags[1] = dat.T
    c3s = c1t - dot_nn(dst, sm) - dot_nn(dat, k2t) - dot_nn(dbt, k1t)
    c3a = c1at - dot_nt(dst, k2t) - dat - dot_nt(dbt, n12t)
    c3b = c1bt - dot_nt(dst, k1t) - dot_nn(dat, n12t) - dbt
    g3 = yy - dot_nt(c1t, dst) - dot_nt(dst, c3s)
    g3 = g3 - dot_nt(c1at, dat) - dot_nt(dat, c3a) - dot_nt(c1bt, dbt) - dot_nt(dbt, c3b)
    lt3, e3 = factor_of(0.5 * (g3 + g3.T))
    uppers[1] = lt3
    e3 = e3 * math.sqrt(size)
    cs[...] = -dot_nn(e3, dst)
    cw[...] = jnp.concatenate(
        [dot_nn(e3, e2), -dot_nn(e3, dot_nn(dat, e2)), -dot_nn(e3, dot_nn(dbt, e1))], axis=1
    )


def small(kernel, name, shapes, *args, flops=10**10):
    return pl.pallas_call(
        kernel,
        out_shape=[jax.ShapeDtypeStruct(s, F32) for s in shapes],
        compiler_params=pltpu.CompilerParams(vmem_limit_bytes=VMEM_LIMIT),
        cost_estimate=pl.CostEstimate(flops=flops, bytes_accessed=2 * 2**20, transcendentals=0),
        name=name,
    )(*args)


def on_device(blocks, pattern, counts, stored, start_block):
    nbd, slots, bs, _ = blocks.shape
    bw, n = start_block.shape
    ks = stored.shape[0]
    devices = lax.axis_size(AXES)
    position = lax.axis_index(AXES)
    nb = nbd * devices
    local = (pattern - (position - 1) * nbd) % nb
    used = jnp.arange(slots, dtype=jnp.int32)[None, :] < counts[:, None]
    plan = make_plan(local, used, nbd)
    tiles = blocks.reshape(nbd * slots, bs, bs)
    up = [(i, (i + 1) % devices) for i in range(devices)]
    down = [(j, i) for i, j in up]

    def halo(w):
        return lax.ppermute(w, AXES, up), lax.ppermute(w, AXES, down)

    half, cut = ks // 2, ks // 4
    upper, lower = stored[:half], stored[half:]
    s11, s12, s22 = dot_nt(upper, upper, HIGH), dot_nt(upper, lower, HIGH), dot_nt(lower, lower, HIGH)
    first = dot_nt(stored, start_block, HIGH)
    packed = [s11[:cut], s12[:cut], s11[cut:, cut:], s12[cut:], s22[:cut], s22[cut:, cut:]]
    packed += [first[q * cut : (q + 1) * cut] for q in range(4)]
    packed = total(jnp.concatenate(packed, axis=1)[:, None])
    wide = (bw, ks)
    s, c1t, minus_dt = small(first_kernel, "first", [(ks, ks), wide, wide], packed)
    w1 = project(minus_dt, jnp.eye(bw, dtype=F32), stored, start_block)
    (c3t,) = small(after_first_kernel, "after_first", [wide], s, c1t, minus_dt, flops=10**8)

    def apply(w, prev):
        left, right = halo(w)
        near, halves, gram = near_op(plan, tiles, w, nbd)
        return far_op(plan, halves, stored, left, right, near, w, prev, gram)

    u1, m1 = apply(w1, w1)
    cs, cw, keep = small(second_kernel, "second", [wide, (bw, 2 * bw), (3 * bw, ks)], total(m1), s, c3t)
    w2 = project(cs, cw, stored, u1, w1)
    (c3,) = small(after_kernel, "after", [(bw, ks + 2 * bw)], s, keep, flops=10**8)

    u2, m2 = apply(w2, w1)
    cs, cw, diags, uppers = small(
        functools.partial(third_kernel, size=nb * bs),
        "third",
        [wide, (bw, 3 * bw), (2, bw, bw), (2, bw, bw)],
        total(m2), s, c3, keep,
    )
    return diags, uppers, project(cs, cw, stored, u2, w2, w1)


def solution(mesh):
    in_specs = (
        P(AXES, None, None, None),
        P(AXES, None),
        P(AXES),
        P(None, AXES),
        P(None, AXES),
    )
    out_specs = (P(), P(), P(None, AXES))
    return jax.shard_map(on_device, mesh=mesh, in_specs=in_specs, out_specs=out_specs, check_vma=False)
```

```python
import functools
import math

import jax
import jax.numpy as jnp
from jax import lax
from jax.experimental import pallas as pl
from jax.experimental.pallas import tpu as pltpu
from jax.sharding import PartitionSpec as P

AXES = ("row", "basis", "rep")
HIGH = lax.Precision.HIGH
FULL = lax.Precision.HIGHEST
F32 = jnp.float32
BF16 = jnp.bfloat16
RB = 4
CHUNK = 8
TILE = 1024
VMEM_LIMIT = 12 * 1024 * 1024


def dot_nt(a, b, precision=FULL):
    return lax.dot_general(a, b, (((1,), (1,)), ((), ())), precision=precision, preferred_element_type=F32)


def dot_tn(a, b, precision=FULL):
    return lax.dot_general(a, b, (((0,), (0,)), ((), ())), precision=precision, preferred_element_type=F32)


def dot_nn(a, b, precision=FULL):
    return lax.dot_general(a, b, (((1,), (0,)), ((), ())), precision=precision, preferred_element_type=F32)


def bdot(a, b):
    return jnp.dot(a, b, preferred_element_type=F32)


def total(x):
    parts = lax.all_to_all(x, AXES, 0, 0, tiled=True)
    mine = jnp.sum(parts, axis=0, keepdims=True)
    return lax.all_to_all(jnp.broadcast_to(mine, x.shape), AXES, 0, 0, tiled=True)[:, 0]


def split(x):
    hi = x.astype(BF16)
    lo = (x - hi.astype(F32)).astype(BF16)
    return hi, lo


def stacked(x):
    return jnp.concatenate(split(x), axis=0)


def bdot_nt(a, b):
    return lax.dot_general(a, b, (((1,), (1,)), ((), ())), preferred_element_type=F32)


def add_slots(plan, first, chunks, size, halves, pieces, tot):
    @pl.loop(0, chunks)
    def _(c):
        parts = []
        for e in range(CHUNK):
            at = first + c * CHUNK + e
            v = pieces[plan[at + 2 * size]]
            parts.append((plan[at + size], bdot_nt(jnp.concatenate([v, v], axis=1), halves[plan[at]])))
        for row, part in parts:
            tot[row] += part


def near_kernel(plan, blocks, mid, tot, halves, gram, pieces):
    nbd, _, bs = tot.shape
    bw, n = mid.shape
    size = plan.shape[0] // 6
    pieces[nbd] = jnp.zeros((2 * bw, bs), BF16)
    tot[...] = jnp.zeros_like(tot)

    @pl.loop(0, nbd, unroll=4)
    def _(b):
        pieces[b] = stacked(mid[:, pl.ds(pl.multiple_of(b * bs, bs), bs)])

    @pl.loop(0, blocks.shape[0], unroll=4)
    def _(k):
        halves[k] = jnp.concatenate(split(blocks[k]), axis=1)

    add_slots(plan, 1, plan[0], size, halves, pieces, tot)
    g = jnp.zeros((bw, 2 * bw), F32)
    for b in range(0, n, TILE):
        hi, lo = split(mid[:, b : b + TILE])
        w = jnp.concatenate([hi, lo], axis=0)
        g = g + bdot_nt(hi, w) + bdot_nt(lo, w)
    gram[...] = g[:, :bw] + g[:, bw:]


def far_kernel(plan, halves, stored, left, right, near, mid, prev, gram, u_out, m_out, tot, pieces, acc, accw):
    nbd, _, bs = tot.shape
    bw, n = mid.shape
    ks = stored.shape[0]
    size = plan.shape[0] // 6
    pieces[2 * nbd] = jnp.zeros((2 * bw, bs), BF16)
    for k, src in enumerate((left, right)):

        @pl.loop(0, nbd, unroll=4)
        def _(b):
            pieces[k * nbd + b] = stacked(src[:, pl.ds(pl.multiple_of(b * bs, bs), bs)])

    tot[...] = jnp.zeros_like(tot)
    add_slots(plan, 3 * size + 1, plan[3 * size], size, halves, pieces, tot)
    acc[...] = jnp.zeros_like(acc)
    accw[...] = jnp.zeros_like(accw)
    per = TILE // bs

    @pl.loop(0, n // TILE)
    def _(b):
        here = pl.ds(pl.multiple_of(b * TILE, TILE), TILE)
        us = []
        for r in range(per):
            t = tot[b * per + r] + near[b * per + r]
            us.append(t[:bw] + t[bw:])
        u = jnp.concatenate(us, axis=1)
        u_out[:, here] = u
        u2 = stacked(u)
        shi, slo = split(stored[:, here])
        acc[...] += bdot_nt(shi, u2) + bdot_nt(slo, u2)
        rhi, rlo = split(jnp.concatenate([mid[:, here], prev[:, here], u], axis=0))
        accw[...] += bdot_nt(rhi, u2) + bdot_nt(rlo, u2)

    t = acc[...].T
    a = t[:bw] + t[bw:]
    m_out[:bw, 0, : ks // 2] = a[:, : ks // 2]
    m_out[bw:, 0, : ks // 2] = a[:, ks // 2 :]
    w = accw[...]
    w = w[:, :bw] + w[:, bw:]
    m_out[:bw, 0, ks // 2 :] = jnp.concatenate([w[:bw], gram[...]], axis=1)
    m_out[bw:, 0, ks // 2 :] = jnp.concatenate([w[bw : 2 * bw], w[2 * bw :]], axis=1)


VMEM = pl.BlockSpec(memory_space=pltpu.VMEM)
SMEM = pl.BlockSpec(memory_space=pltpu.SMEM)


def near_op(plan, blocks, mid, nbd):
    _, bs, _ = blocks.shape
    bw, n = mid.shape
    return pl.pallas_call(
        near_kernel,
        in_specs=[SMEM, VMEM, VMEM],
        out_specs=[VMEM] * 3,
        out_shape=[
            jax.ShapeDtypeStruct((nbd, 2 * bw, bs), F32),
            jax.ShapeDtypeStruct((blocks.shape[0], bs, 2 * bs), BF16),
            jax.ShapeDtypeStruct((bw, bw), F32),
        ],
        scratch_shapes=[pltpu.VMEM((nbd + 1, 2 * bw, bs), BF16)],
        compiler_params=pltpu.CompilerParams(vmem_limit_bytes=VMEM_LIMIT),
        cost_estimate=pl.CostEstimate(flops=2 * 10**9, bytes_accessed=12 * 2**20, transcendentals=0),
        name="near_op",
    )(plan, blocks, mid)


def far_op(plan, halves, stored, left, right, near, mid, prev, gram):
    nbd, _, bs = near.shape
    bw, n = mid.shape
    ks = stored.shape[0]
    return pl.pallas_call(
        far_kernel,
        in_specs=[SMEM] + [VMEM] * 8,
        out_specs=[VMEM] * 2,
        scratch_shapes=[
            pltpu.VMEM((nbd, 2 * bw, bs), F32),
            pltpu.VMEM((2 * nbd + 1, 2 * bw, bs), BF16),
            pltpu.VMEM((ks, 2 * bw), F32),
            pltpu.VMEM((3 * bw, 2 * bw), F32),
        ],
        out_shape=[
            jax.ShapeDtypeStruct((bw, n), F32),
            jax.ShapeDtypeStruct((2 * bw, 1, ks // 2 + 2 * bw), F32),
        ],
        compiler_params=pltpu.CompilerParams(vmem_limit_bytes=VMEM_LIMIT),
        cost_estimate=pl.CostEstimate(flops=2 * 10**9, bytes_accessed=20 * 2**20, transcendentals=0),
        name="far_op",
    )(plan, halves, stored, left, right, near, mid, prev, gram)


def make_plan(local, used, nbd):
    slots = local.shape[1]
    total_slots = nbd * slots
    size = -(-total_slots // CHUNK) * CHUNK + 1
    local, used = local.reshape(-1), used.reshape(-1)
    mine = (local >= nbd) & (local < 2 * nbd)
    ids = jnp.arange(total_slots, dtype=jnp.int32)
    rows = jnp.arange(size - 1, dtype=jnp.int32)
    out = []
    for flag, piece, empty in (
        (used & mine, local - nbd, nbd),
        (used & ~mine, jnp.where(local < nbd, local, local - nbd), 2 * nbd),
    ):
        before = jnp.sum(((ids[None, :] < ids[:, None]) & flag[None, :]).astype(jnp.int32), axis=1)
        hit = (before[None, :] == rows[:, None]) & flag[None, :]
        count = jnp.sum(flag.astype(jnp.int32))
        slot = jnp.sum(jnp.where(hit, ids[None, :], 0), axis=1)
        where = jnp.sum(jnp.where(hit, piece[None, :], 0), axis=1)
        where = jnp.where(rows < count, where, empty)
        zero = jnp.zeros((1,), jnp.int32)
        chunks = (count + CHUNK - 1) // CHUNK
        out += [chunks[None], slot, zero, slot // slots, zero, where]
    return jnp.concatenate(out)


def project_kernel(cs, cw, stored, *refs):
    arrays, out = refs[:-1], refs[-1]
    bw, n = out.shape
    chi, clo = split(jnp.concatenate([cs[...], cw[...]], axis=1))
    c2 = jnp.concatenate([chi, clo], axis=0)

    @pl.loop(0, n // TILE)
    def _(i):
        here = pl.ds(pl.multiple_of(i * TILE, TILE), TILE)
        dhi, dlo = split(jnp.concatenate([stored[:, here]] + [a[:, here] for a in arrays], axis=0))
        t = bdot(c2, dhi)
        out[:, here] = t[:bw] + t[bw:] + bdot(chi, dlo)


def project(cs, cw, stored, *arrays):
    vmem = pl.BlockSpec(memory_space=pltpu.VMEM)
    return pl.pallas_call(
        project_kernel,
        in_specs=[vmem] * (3 + len(arrays)),
        out_specs=vmem,
        out_shape=jax.ShapeDtypeStruct(arrays[0].shape, F32),
        compiler_params=pltpu.CompilerParams(vmem_limit_bytes=VMEM_LIMIT),
        name="project",
    )(cs, cw, stored, *arrays)


PANEL = 16


def factor_of(gram):
    n = gram.shape[0]
    row = lax.broadcasted_iota(jnp.int32, (n, 2 * n), 0)
    lane = lax.broadcasted_iota(jnp.int32, (n, 2 * n), 1)
    eye = (lane == row + n).astype(F32)
    m = jnp.where(lane < n, jnp.concatenate([gram, gram], axis=1), eye)
    pivots = jnp.ones((n, 2 * n), F32)
    for p in range(0, n, PANEL):
        cols = [jnp.broadcast_to(m[:, p + j : p + j + 1], (n, 2 * n)) for j in range(PANEL)]
        for j in range(PANEL):
            k = p + j
            pivot = cols[j][k : k + 1]
            inv = pl.reciprocal(pivot, approx=True)
            inv = inv * (2.0 - pivot * inv)
            inv = inv * (2.0 - pivot * inv)
            pivots = jnp.where(row == k, pivot, pivots)
            f = jnp.where(row > k, cols[j], 0.0) * inv
            for q in range(j + 1, PANEL):
                cols[q] = cols[q] - f * cols[q][k : k + 1]
            m = m - f * m[k : k + 1]
    root = lax.rsqrt(pivots)
    m = m * (root * (1.5 - 0.5 * pivots * root * root))
    upper = jnp.where(lane >= row, m, 0.0)[:, :n]
    return upper, m[:, n:]


def unpacked(t, bw):
    half = t.shape[1] - 2 * bw
    mst = jnp.concatenate([t[:bw, :half], t[bw:, :half]], axis=1)
    a = t[:bw, half:]
    b = t[bw:, half:]
    return mst, a[:, :bw], a[:, bw:], b[:, :bw], b[:, bw:]


def first_kernel(packed, s, c1t_out, minus_dt):
    bw, ks = c1t_out.shape
    cut = ks // 4
    at = 0
    for q in range(4):
        for k in range(q, 4):
            block = packed[:, at : at + cut]
            at += cut
            s[q * cut : (q + 1) * cut, k * cut : (k + 1) * cut] = block
            if k > q:
                s[k * cut : (k + 1) * cut, q * cut : (q + 1) * cut] = block.T
    t = packed[:, at:].T
    c1t = jnp.concatenate([t[q * bw : (q + 1) * bw] for q in range(4)], axis=1)
    c1t_out[...] = c1t
    minus_dt[...] = dot_nn(c1t, s[...]) - 2.0 * c1t


def after_first_kernel(s, c1t, minus_dt, c3t):
    c3t[...] = c1t[...] + dot_nn(minus_dt[...], s[...])


def second_kernel(t, s, c3t, cs, cw, keep):
    bw = c3t.shape[0]
    mst, h, g, _, _ = unpacked(t[...], bw)
    _, e1 = factor_of(g)
    k1t = dot_nn(e1, c3t[...])
    c1t = dot_nn(e1, mst)
    c1vt = dot_nt(e1, dot_nn(e1, h))
    c2t = c1t - dot_nn(c1t, s[...]) - dot_nn(c1vt, k1t)
    c2vt = -dot_nt(c1t, k1t)
    dvt = c1vt + c2vt
    cs[...] = -(c1t + c2t)
    cw[...] = jnp.concatenate([e1, -dot_nn(dvt, e1)], axis=1)
    keep[:bw] = k1t
    keep[bw : 2 * bw] = c2t
    keep[2 * bw :, : 4 * bw] = jnp.concatenate([e1, c2vt, dvt.T, dvt], axis=1)


def after_kernel(s, keep, c3):
    bw = c3.shape[0]
    k1t, c2t, c2vt = keep[:bw], keep[bw : 2 * bw], keep[2 * bw :, bw : 2 * bw]
    c3[:, : s.shape[0]] = c2t - dot_nn(c2t, s[...]) - dot_nn(c2vt, k1t)
    c3vt = -dot_nt(c2t, k1t)
    c3[:, s.shape[0] :] = jnp.concatenate([c3vt, c3vt], axis=1)


def third_kernel(t, s, c3, keep, cs, cw, diags, uppers, *, size):
    bw = c3.shape[0]
    sm = s[...]
    k1t, e1 = keep[:bw], keep[2 * bw :, :bw]
    c3st, c3vt = c3[:, : sm.shape[0]], c3[:, sm.shape[0] : sm.shape[0] + bw]
    mst, h, g, h12, uu = unpacked(t[...], bw)
    lt2, e2 = factor_of(g)
    uppers[0] = lt2
    k2t = dot_nn(e2, c3st)
    n12t = dot_nn(e2, c3vt)
    c1t = dot_nn(e2, mst)
    c1at = dot_nt(e2, dot_nn(e2, h))
    c1bt = dot_nt(e2, dot_nn(e1, h12))
    yy = dot_nt(dot_nn(e2, uu), e2)
    dst = 2.0 * c1t - dot_nn(c1t, sm) - dot_nn(c1at, k2t) - dot_nn(c1bt, k1t)
    dat = c1at - dot_nt(c1t, k2t) - dot_nt(c1bt, n12t)
    dbt = c1bt - dot_nt(c1t, k1t) - dot_nn(c1at, n12t)
    diags[0] = keep[2 * bw :, 2 * bw : 3 * bw]
    diags[1] = dat.T
    c3s = c1t - dot_nn(dst, sm) - dot_nn(dat, k2t) - dot_nn(dbt, k1t)
    c3a = c1at - dot_nt(dst, k2t) - dat - dot_nt(dbt, n12t)
    c3b = c1bt - dot_nt(dst, k1t) - dot_nn(dat, n12t) - dbt
    g3 = yy - dot_nt(c1t, dst) - dot_nt(dst, c3s)
    g3 = g3 - dot_nt(c1at, dat) - dot_nt(dat, c3a) - dot_nt(c1bt, dbt) - dot_nt(dbt, c3b)
    lt3, e3 = factor_of(0.5 * (g3 + g3.T))
    uppers[1] = lt3
    e3 = e3 * math.sqrt(size)
    cs[...] = -dot_nn(e3, dst)
    cw[...] = jnp.concatenate(
        [dot_nn(e3, e2), -dot_nn(e3, dot_nn(dat, e2)), -dot_nn(e3, dot_nn(dbt, e1))], axis=1
    )


def small(kernel, name, shapes, *args, flops=10**10):
    return pl.pallas_call(
        kernel,
        out_shape=[jax.ShapeDtypeStruct(s, F32) for s in shapes],
        compiler_params=pltpu.CompilerParams(vmem_limit_bytes=VMEM_LIMIT),
        cost_estimate=pl.CostEstimate(flops=flops, bytes_accessed=2 * 2**20, transcendentals=0),
        name=name,
    )(*args)


def on_device(blocks, pattern, counts, stored, start_block):
    nbd, slots, bs, _ = blocks.shape
    bw, n = start_block.shape
    ks = stored.shape[0]
    devices = lax.axis_size(AXES)
    position = lax.axis_index(AXES)
    nb = nbd * devices
    local = (pattern - (position - 1) * nbd) % nb
    used = jnp.arange(slots, dtype=jnp.int32)[None, :] < counts[:, None]
    plan = make_plan(local, used, nbd)
    tiles = blocks.reshape(nbd * slots, bs, bs)
    up = [(i, (i + 1) % devices) for i in range(devices)]
    down = [(j, i) for i, j in up]

    def halo(w):
        return lax.ppermute(w, AXES, up), lax.ppermute(w, AXES, down)

    half, cut = ks // 2, ks // 4
    upper, lower = stored[:half], stored[half:]
    top, s22 = dot_nt(upper, stored, HIGH), dot_nt(lower, lower, HIGH)
    s11, s12 = top[:, :half], top[:, half:]
    first = dot_nt(stored, start_block, HIGH)
    packed = [s11[:cut], s12[:cut], s11[cut:, cut:], s12[cut:], s22[:cut], s22[cut:, cut:]]
    packed += [first[q * cut : (q + 1) * cut] for q in range(4)]
    packed = total(jnp.concatenate(packed, axis=1)[:, None])
    wide = (bw, ks)
    s, c1t, minus_dt = small(first_kernel, "first", [(ks, ks), wide, wide], packed)
    w1 = project(minus_dt, jnp.eye(bw, dtype=F32), stored, start_block)
    (c3t,) = small(after_first_kernel, "after_first", [wide], s, c1t, minus_dt, flops=10**8)

    def apply(w, prev):
        left, right = halo(w)
        near, halves, gram = near_op(plan, tiles, w, nbd)
        return far_op(plan, halves, stored, left, right, near, w, prev, gram)

    u1, m1 = apply(w1, w1)
    cs, cw, keep = small(second_kernel, "second", [wide, (bw, 2 * bw), (3 * bw, ks)], total(m1), s, c3t)
    w2 = project(cs, cw, stored, u1, w1)
    (c3,) = small(after_kernel, "after", [(bw, ks + 2 * bw)], s, keep, flops=10**8)

    u2, m2 = apply(w2, w1)
    cs, cw, diags, uppers = small(
        functools.partial(third_kernel, size=nb * bs),
        "third",
        [wide, (bw, 3 * bw), (2, bw, bw), (2, bw, bw)],
        total(m2), s, c3, keep,
    )
    return diags, uppers, project(cs, cw, stored, u2, w2, w1)


def solution(mesh):
    in_specs = (
        P(AXES, None, None, None),
        P(AXES, None),
        P(AXES),
        P(None, AXES),
        P(None, AXES),
    )
    out_specs = (P(), P(), P(None, AXES))
    return jax.shard_map(on_device, mesh=mesh, in_specs=in_specs, out_specs=out_specs, check_vma=False)
```
